32 devices in a mesh: comp: 8 (over y, x, core), dom: 4 (over z).
Axes of the slice: x: 2, y: 2, z: 4, core: 2. Of those that a mesh axis runs over, the one named last changes fastest.
Arguments:
- density: float32 [8, 32, 16, 16, 256], P('comp', 'dom'), may hold values from -6 to 6
- velocity: bfloat16 [8, 6, 32, 16, 16, 256], P('comp', None, 'dom'), may hold values from -0.099609375 to 0.099609375
- coefficients: int32 [8], replicated, may hold values from -1 to 1, as said below
- owner_lists: int32 [196, 8], replicated, may hold values from -1 to 255, as said below
Outputs:
- combined: float32 [8, 32, 16, 16, 256], P('comp', 'dom')
The draws below stay inside these ranges and needn't reach their ends.
Inputs may be any that keep to these rules, and one draw needn't show every extreme that they name: `coefficients`: each is -1 or 1. `owner_lists`: every slab number c * 32 + s appears in exactly one row; within a row the entries are distinct and ascending, padding -1 follows them, and every row has at least one entry; no row names two slabs of one component; 4 rows name all 8 components; exactly 36 rows have more than one entry, and those that do not name all components have exactly two; every component has exactly 12 slabs in rows with more than one entry.
All inputs are finite; a program needn't handle non-finite values.
Results may differ from the reference program's by a relative error of at most 0.0003.
Values may be sent and summed in bfloat16 or wider, within the bound.
No kernel may reach another device: no remote copies, remote signals or barrier semaphores. Data moves between devices by JAX's collectives and lax.ppermute only.
A program may use at most 128 MiB of HBM per device.

```python
import jax
import jax.numpy as jnp
import numpy as np
from jax import lax

GRID_A = 32
GRID_B = 16
GRID_C = 16
GRID_D = 8
GRID_E = 8
GRID_F = 4
STEPS = 4
SHARED = 4
BORROWED = 4
COMPS = 8
OWN_SLABS = 24
SUBSPACE_BLOCKS = 196


def slab_labels(key):
    comp_order = jax.random.permutation(jax.random.fold_in(key, 2), COMPS).astype(jnp.int32)
    comp_place = jnp.zeros((COMPS,), jnp.int32).at[comp_order].set(jnp.arange(COMPS, dtype=jnp.int32))
    offsets = (jax.random.permutation(jax.random.fold_in(key, 3), COMPS - 1)[:BORROWED] + 1).astype(jnp.int32)

    def for_component(component):
        comp_key = jax.random.fold_in(key, component)
        ordering = jax.random.permutation(jax.random.fold_in(comp_key, 1), GRID_A)
        roles = jnp.arange(GRID_A, dtype=jnp.int32)
        borrowed_index = jnp.clip(roles - SHARED - OWN_SLABS, 0, BORROWED - 1)

        def destination_for(lent_index):
            return comp_order[(comp_place[component] + offsets[lent_index]) % COMPS]

        def pick_for(lent_index):
            lent_target = destination_for(lent_index)
            chosen = jax.random.permutation(jax.random.fold_in(key, 1000 + lent_target), OWN_SLABS)
            return chosen[lent_index].astype(jnp.int32)
        lent_indices = jnp.arange(BORROWED, dtype=jnp.int32)
        targets = jax.vmap(destination_for)(lent_indices)
        picks = jax.vmap(pick_for)(lent_indices)
        own_label = SHARED + component * OWN_SLABS + roles - SHARED
        lent_label = SHARED + targets[borrowed_index] * OWN_SLABS + picks[borrowed_index]
        label = jnp.where(roles < SHARED, roles, jnp.where(roles < SHARED + OWN_SLABS, own_label, lent_label))
        return jnp.zeros((GRID_A,), jnp.int32).at[ordering].set(label.astype(jnp.int32))
    block_labels = jax.vmap(for_component)(jnp.arange(COMPS, dtype=jnp.int32)).reshape(-1)
    relabel_blocks = jax.random.permutation(jax.random.fold_in(key, 4), SUBSPACE_BLOCKS).astype(jnp.int32)
    return relabel_blocks[block_labels]


def draw_owner_lists(key, part):
    block_labels = slab_labels(jax.random.fold_in(key, 11))
    blocks = jnp.arange(SUBSPACE_BLOCKS, dtype=jnp.int32)
    hits = block_labels[None, :] == blocks[:, None]
    ranking = jnp.argsort(jnp.where(hits, 0, 1).astype(jnp.int32), axis=1, stable=True)[:, :COMPS]
    counts = jnp.sum(hits.astype(jnp.int32), axis=1)
    slots = jnp.arange(COMPS, dtype=jnp.int32)
    return jnp.where(slots[None, :] < counts[:, None], ranking, -1).astype(jnp.int32)


def draw_coefficients(key, part):
    return (2 * jax.random.randint(jax.random.fold_in(key, 7), (COMPS,), 0, 2) - 1).astype(jnp.int32)


def shard_levels(stream_key, shape, cuts, low, top_value):
    def one(axis_at, shards_of):
        draws = jax.random.uniform(jax.random.fold_in(jax.random.fold_in(stream_key, 6), axis_at), (shards_of,), jnp.float32, low / len(cuts), top_value / len(cuts))
        return jnp.repeat(jnp.exp(draws), shape[axis_at] // shards_of).reshape((-1,) + (1,) * (len(shape) - axis_at - 1))

    factor_of = one(*cuts[0])
    for cut in cuts[1:]:
        factor_of = factor_of * one(*cut)
    return factor_of


def gaussian(rng, shape, width, reach, cuts=(), kind=jnp.bfloat16):
    level = shard_levels(rng, shape, cuts, -0.22, 0.18) if cuts else 1.0
    values = jax.random.normal(rng, shape, jnp.float32) * width * level
    return jnp.minimum(jnp.maximum(values, -reach), reach).astype(kind)


def setup_inputs(seed: int = 0) -> dict:
    streams_of = jax.random.split(jax.random.key(seed), 5)
    return {
        "density": gaussian(streams_of[0], (COMPS, GRID_A, GRID_B, GRID_C, GRID_D * GRID_E * GRID_F), 1.0, 6.0, ((0, 8), (1, 4)), jnp.float32),
        "velocity": jnp.clip(jax.random.uniform(streams_of[1], (COMPS, 6, GRID_A, GRID_B, GRID_C, GRID_D * GRID_E * GRID_F), jnp.float32, -0.099609375, 0.099609375) * shard_levels(streams_of[1], (COMPS, 6, GRID_A, GRID_B, GRID_C, GRID_D * GRID_E * GRID_F), ((0, 8), (2, 4)), -0.4, 0.0), -0.099609375, 0.099609375).astype(jnp.bfloat16),
        "coefficients": draw_coefficients(jax.random.fold_in(streams_of[4], 71), 0),
        "owner_lists": draw_owner_lists(jax.random.fold_in(streams_of[4], 71), 0),
    }


def surplus_matrix(points):
    matrix = np.eye(points)
    for position in range(1, points):
        spacing = position & (-position)
        matrix[position, (position - spacing) % points] -= 0.5
        matrix[position, (position + spacing) % points] -= 0.5
    return matrix


def nodal_matrix(points):
    matrix = np.zeros((points, points))
    matrix[0, 0] = 1.0
    spacing = points // 2
    while spacing >= 1:
        for position in range(spacing, points, 2 * spacing):
            matrix[position] = 0.5 * (matrix[(position - spacing) % points] + matrix[(position + spacing) % points])
            matrix[position, position] += 1.0
        spacing = spacing // 2
    return matrix


def along_axis(values, matrix, dimension):
    moved = jnp.tensordot(values, jnp.asarray(matrix, values.dtype), axes=([dimension], [1]), precision=lax.Precision.HIGHEST)
    return jnp.moveaxis(moved, -1, dimension)


def advance(values, speeds):
    full_shape = (COMPS, GRID_A, GRID_B, GRID_C, GRID_D, GRID_E, GRID_F)
    current = values.reshape(full_shape)
    rates = speeds.astype(values.dtype).reshape((COMPS, 6) + full_shape[1:])
    updated = current
    for dimension in range(6):
        forward_sweep = jnp.roll(current, -1, dimension + 1)
        backward = jnp.roll(current, 1, dimension + 1)
        updated = updated + 0.06 * (forward_sweep - 2.0 * current + backward) - 0.5 * rates[:, dimension] * (forward_sweep - backward)
    return updated.reshape(values.shape)


def slab_blocks(owner_lists):
    block_labels = jnp.broadcast_to(jnp.arange(SUBSPACE_BLOCKS, dtype=jnp.int32)[:, None], owner_lists.shape)
    targets = jnp.where(owner_lists >= 0, owner_lists, COMPS * GRID_A).astype(jnp.int32)
    empty = jnp.zeros((COMPS * GRID_A,), jnp.int32)
    return empty.at[targets.reshape(-1)].set(block_labels.reshape(-1), mode="drop")


def reference(density, velocity, coefficients, owner_lists):
    advected = density
    for time_step in range(STEPS):
        advected = advance(advected, velocity)
    inner_surplus = np.kron(np.kron(surplus_matrix(GRID_D), surplus_matrix(GRID_E)), surplus_matrix(GRID_F))
    surplus = along_axis(advected, inner_surplus, 4)
    surplus = along_axis(surplus, surplus_matrix(GRID_B), 2)
    surplus = along_axis(surplus, surplus_matrix(GRID_C), 3)
    surplus = along_axis(surplus, surplus_matrix(GRID_A), 1)
    slab_rows = surplus.reshape(COMPS * GRID_A, -1)
    weights = jnp.repeat(coefficients.astype(density.dtype), GRID_A)
    block_of = slab_blocks(owner_lists)
    block_sum = jax.ops.segment_sum(slab_rows * weights[:, None], block_of, num_segments=SUBSPACE_BLOCKS)
    merged = block_sum[block_of].reshape(surplus.shape)
    inner_nodal = np.kron(np.kron(nodal_matrix(GRID_D), nodal_matrix(GRID_E)), nodal_matrix(GRID_F))
    result = along_axis(merged, nodal_matrix(GRID_A), 1)
    result = along_axis(result, inner_nodal, 4)
    result = along_axis(result, nodal_matrix(GRID_B), 2)
    result = along_axis(result, nodal_matrix(GRID_C), 3)
    return result
```

```python
import jax
import jax.numpy as jnp
from jax import lax
from jax.experimental import pallas as pl
from jax.experimental.pallas import tpu as pltpu
from jax.sharding import PartitionSpec as P

GRID_A = 32
GRID_B = 16
GRID_C = 16
LANES = 256
HALF = 128
D_STRIDE = 32
E_STRIDE = 4
F_EXTENT = 4
STEPS = 4
SHARED = 4
BORROWED = 4
MULTI = 12
LEVELS = 32000.0
FINE = 16.0
TINY = 1e-36
VMEM_LIMIT = 48 * 1024 * 1024


def params():
    return pltpu.CompilerParams(vmem_limit_bytes=VMEM_LIMIT)


def smem():
    return pl.BlockSpec(memory_space=pltpu.SMEM)


def whole(shape):
    return pl.BlockSpec(shape, lambda *_: (0,) * len(shape))


def code_of(peak):
    return jnp.ceil(jnp.log(jnp.maximum(peak, TINY)) * (FINE / 0.6931471805599453))


def encode(rows, put, put_code):
    peak = jnp.abs(rows[0]())
    for row in rows[1:]:
        peak = jnp.maximum(peak, jnp.abs(row()))
    code = code_of(peak)
    factor = jnp.exp2(code * (-1.0 / FINE)) * LEVELS
    put_code(code.astype(jnp.int32).astype(jnp.int16))
    for index, row in enumerate(rows):
        put(index, jnp.round(row() * factor).astype(jnp.int32).astype(jnp.int16))


def to_float(block):
    return block.astype(jnp.int32).astype(jnp.float32)


def unit_of(code_row):
    return jnp.exp2(to_float(code_row) * (1.0 / FINE)) * (1.0 / LEVELS)


def send_planes_body(first, last, out_first, out_last):
    for source, out in ((first, out_first), (last, out_last)):
        rows = [lambda b=b, source=source: source[0, 0, b] for b in range(GRID_B)]
        encode(
            rows,
            lambda b, value, out=out: out.__setitem__(b, value),
            lambda value, out=out: out.__setitem__(GRID_B, value),
        )


def message_shape():
    return jax.ShapeDtypeStruct((GRID_B + 1, GRID_C, LANES), jnp.int16)


def send_planes(density):
    planes = density.shape[1]
    block = (1, 1, GRID_B, GRID_C, LANES)
    return pl.pallas_call(
        send_planes_body,
        grid=(1,),
        in_specs=[
            pl.BlockSpec(block, lambda i: (0, 0, 0, 0, 0)),
            pl.BlockSpec(block, lambda i: (0, planes - 1, 0, 0, 0)),
        ],
        out_specs=[whole(message_shape().shape)] * 2,
        out_shape=[message_shape()] * 2,
        compiler_params=params(),
    )(density, density)


def stencil_rest(value, after, before, rates):
    lane = lax.broadcasted_iota(jnp.int32, (GRID_C, HALF), 1)
    left, right = value[:, :HALF], value[:, HALF:]

    def lane_pair(extent, stride):
        position = lane // stride % extent
        wrap = (extent - 1) * stride
        forward, backward = [], []
        for half in (left, right):
            forward.append(
                jnp.where(
                    position == extent - 1,
                    pltpu.roll(half, wrap, 1),
                    pltpu.roll(half, HALF - stride, 1),
                )
            )
            backward.append(
                jnp.where(
                    position == 0,
                    pltpu.roll(half, HALF - wrap, 1),
                    pltpu.roll(half, stride, 1),
                )
            )
        return jnp.concatenate(forward, 1), jnp.concatenate(backward, 1)

    pairs = [
        (after, before),
        (pltpu.roll(value, GRID_C - 1, 0), pltpu.roll(value, 1, 0)),
        (pltpu.roll(value, LANES - D_STRIDE, 1), pltpu.roll(value, D_STRIDE, 1)),
        lane_pair(D_STRIDE // E_STRIDE, E_STRIDE),
        lane_pair(F_EXTENT, 1),
    ]
    total = 0.28 * value
    for (forward, backward), rate in zip(pairs, rates):
        total = total + 0.06 * (forward + backward) - (0.5 * rate) * (forward - backward)
    return total


def inner_body(grid, speeds, out):
    plane = pl.program_id(0) + 1

    def row(b, carry):
        value = grid[plane, b]
        rates = [speeds[0, d, 0, b].astype(jnp.float32) for d in range(6)]
        rest = stencil_rest(
            value,
            grid[plane, lax.rem(b + 1, GRID_B)],
            grid[plane, lax.rem(b + GRID_B - 1, GRID_B)],
            rates[1:],
        )
        forward, backward = grid[plane + 1, b], grid[plane - 1, b]
        out[0, b] = rest + 0.06 * (forward + backward) - (0.5 * rates[0]) * (forward - backward)
        return carry

    lax.fori_loop(0, GRID_B, row, 0, unroll=2)


def inner_planes(grid, velocity):
    planes = grid.shape[0]
    points = (planes - 2) * GRID_B * GRID_C * LANES
    return pl.pallas_call(
        inner_body,
        grid=(planes - 2,),
        in_specs=[
            whole(grid.shape),
            pl.BlockSpec((1, 6, 1, GRID_B, GRID_C, LANES), lambda p: (0, 0, p + 1, 0, 0, 0)),
        ],
        out_specs=pl.BlockSpec((1, GRID_B, GRID_C, LANES), lambda p: (p + 1, 0, 0, 0)),
        out_shape=jax.ShapeDtypeStruct(grid.shape, jnp.float32),
        compiler_params=params(),
        cost_estimate=pl.CostEstimate(
            flops=40 * points, bytes_accessed=20 * points, transcendentals=0
        ),
    )(grid, velocity)


def edge_body(message, mid, near, low, high, speeds, partial, out, *rest):
    del partial
    *messages, halo = rest
    side = pl.program_id(0)

    def unpack(source):
        unit = unit_of(source[GRID_B])
        for b in range(GRID_B):
            halo[b] = to_float(source[b]) * unit

    @pl.when(side == 0)
    def _():
        unpack(low)

    @pl.when(side == 1)
    def _():
        unpack(high)

    sign = jnp.where(side == 0, -0.5, 0.5)

    def row(b, carry):
        value = mid[0, b]
        rates = [speeds[0, d, 0, b].astype(jnp.float32) for d in range(6)]
        part = stencil_rest(
            value,
            mid[0, lax.rem(b + 1, GRID_B)],
            mid[0, lax.rem(b + GRID_B - 1, GRID_B)],
            rates[1:],
        )
        outer, inside = halo[b], near[0, b]
        out[0, b] = part + 0.06 * (outer + inside) - (sign * rates[0]) * (outer - inside)
        return carry

    lax.fori_loop(0, GRID_B, row, 0, unroll=2)
    if message:
        rows = [lambda b=b: out[0, b] for b in range(GRID_B)]
        for which, target in enumerate(messages):

            @pl.when(side == which)
            def _(target=target):
                encode(
                    rows,
                    lambda b, value: target.__setitem__(b, value),
                    lambda value: target.__setitem__(GRID_B, value),
                )


def edge_planes(grid, low, high, velocity, partial, message):
    planes = grid.shape[0]
    plane = (1, GRID_B, GRID_C, LANES)
    points = 2 * GRID_B * GRID_C * LANES
    out_specs = [pl.BlockSpec(plane, lambda i: (i * (planes - 1), 0, 0, 0))]
    out_shape = [jax.ShapeDtypeStruct(grid.shape, jnp.float32)]
    if message:
        out_specs += [whole(message_shape().shape)] * 2
        out_shape += [message_shape()] * 2
    return pl.pallas_call(
        lambda *refs: edge_body(message, *refs),
        grid=(2,),
        in_specs=[
            pl.BlockSpec(plane, lambda i: (i * (planes - 1), 0, 0, 0)),
            pl.BlockSpec(plane, lambda i: (1 + i * (planes - 3), 0, 0, 0)),
            whole(message_shape().shape),
            whole(message_shape().shape),
            pl.BlockSpec(
                (1, 6, 1, GRID_B, GRID_C, LANES), lambda i: (0, 0, i * (planes - 1), 0, 0, 0)
            ),
            pl.BlockSpec(memory_space=pl.ANY),
        ],
        out_specs=out_specs,
        out_shape=out_shape,
        scratch_shapes=[pltpu.VMEM((GRID_B, GRID_C, LANES), jnp.float32)],
        input_output_aliases={5: 0},
        compiler_params=params(),
        cost_estimate=pl.CostEstimate(
            flops=50 * points, bytes_accessed=24 * points, transcendentals=0
        ),
    )(grid, grid, low, high, velocity, partial)


def spread_body(grid, out):
    planes, width = grid.shape[0], grid.shape[1]
    rows = [
        lambda p=p, b=b: grid[p, b] for p in range(planes) for b in range(width)
    ]
    encode(
        rows,
        lambda index, value: out.__setitem__((0, index), value),
        lambda value: out.__setitem__((0, len(rows)), value),
    )


def spread_columns(grid, dom_count):
    planes, width = grid.shape[0], GRID_B // dom_count
    shape = (dom_count, planes * width + 1, GRID_C, LANES)
    return pl.pallas_call(
        spread_body,
        grid=(dom_count,),
        in_specs=[pl.BlockSpec((planes, width, GRID_C, LANES), lambda e: (0, e, 0, 0))],
        out_specs=pl.BlockSpec((1,) + shape[1:], lambda e: (e, 0, 0, 0)),
        out_shape=jax.ShapeDtypeStruct(shape, jnp.int16),
        compiler_params=params(),
    )(grid)


def chunk_slices(comp_count, width):
    splits = comp_count // (2 * width)
    extent = GRID_C // splits
    chunks = []
    for b in range(width):
        for half in range(2):
            for part in range(splits):
                chunks.append(
                    (b, slice(part * extent, (part + 1) * extent), slice(half * HALF, (half + 1) * HALF))
                )
    return chunks, extent


def surplus_body(chunks, width, slabs, weight, columns, out, rows):
    planes = GRID_A // columns.shape[0]
    last = columns.shape[1] - 1

    def one(index, carry):
        total = [None] * width
        share = jnp.where(slabs[0, index] > 0, -0.5 * weight[0], 0.0)
        for kind in range(3):
            slab = slabs[kind, index]
            source, plane = lax.div(slab, planes), lax.rem(slab, planes)
            unit = unit_of(columns[source, last]) * (weight[0] if kind == 0 else share)
            for b in range(width):
                term = to_float(columns[source, plane * width + b]) * unit
                total[b] = term if kind == 0 else total[b] + term
        for b in range(width):
            rows[index, b] = total[b]
        return carry

    lax.fori_loop(0, MULTI, one, 0)
    for which, (b, third, lanes) in enumerate(chunks):
        readers = [
            lambda i=i, b=b, third=third, lanes=lanes: rows[i, b, third, lanes]
            for i in range(MULTI)
        ]
        encode(
            readers,
            lambda index, value, which=which: out.__setitem__((which, index), value),
            lambda value, which=which: out.__setitem__((which, MULTI), value),
        )


def surplus_rows(columns, slabs, weight, comp_count):
    width = GRID_B // columns.shape[0]
    chunks, extent = chunk_slices(comp_count, width)
    shape = (comp_count, MULTI + 1, extent, HALF)
    return pl.pallas_call(
        lambda *refs: surplus_body(chunks, width, *refs),
        in_specs=[smem(), smem(), whole(columns.shape)],
        out_specs=whole(shape),
        grid=(1,),
        out_shape=jax.ShapeDtypeStruct(shape, jnp.int16),
        scratch_shapes=[pltpu.VMEM((MULTI, width, GRID_C, LANES), jnp.float32)],
        compiler_params=params(),
    )(slabs, weight, columns)


def merge_body(blocks, terms, out, sums, rows):
    comp_count = terms.shape[0]
    sums[...] = jnp.zeros_like(sums)
    for comp in range(comp_count):
        unit = unit_of(terms[comp, MULTI])
        for index in range(MULTI):
            value = to_float(terms[comp, index]) * unit
            rows[comp, index] = value
            block = blocks[comp, index]
            sums[block] = sums[block] + value
    for comp in range(comp_count):
        for index in range(MULTI):
            rows[comp, index] = sums[blocks[comp, index]] - rows[comp, index]
        readers = [lambda i=i, comp=comp: rows[comp, i] for i in range(MULTI)]
        encode(
            readers,
            lambda index, value, comp=comp: out.__setitem__((comp, index), value),
            lambda value, comp=comp: out.__setitem__((comp, MULTI), value),
        )


def merge_rows(terms, blocks):
    comp_count, _, extent, lanes = terms.shape
    return pl.pallas_call(
        merge_body,
        in_specs=[smem(), whole(terms.shape)],
        out_specs=whole(terms.shape),
        grid=(1,),
        out_shape=jax.ShapeDtypeStruct(terms.shape, jnp.int16),
        scratch_shapes=[
            pltpu.VMEM((SHARED + comp_count * BORROWED, extent, lanes), jnp.float32),
            pltpu.VMEM((comp_count, MULTI, extent, lanes), jnp.float32),
        ],
        compiler_params=params(),
    )(blocks, terms)


def nodal_body(chunks, width, slabs, terms, out, grid):
    dom_count = out.shape[0]
    planes = GRID_A // dom_count
    grid[...] = jnp.zeros_like(grid)
    for which, (b, third, lanes) in enumerate(chunks):
        unit = unit_of(terms[which, MULTI])
        for index in range(MULTI):
            grid[slabs[0, index], b, third, lanes] = to_float(terms[which, index]) * unit

    def column(b, carry):
        spacing = GRID_A // 2
        while spacing >= 1:
            for position in range(spacing, GRID_A, 2 * spacing):
                grid[position, b] = grid[position, b] + 0.5 * (
                    grid[position - spacing, b] + grid[(position + spacing) % GRID_A, b]
                )
            spacing //= 2
        return carry

    lax.fori_loop(0, width, column, 0)

    def target(dom, carry):
        rows = [
            lambda p=p, b=b: grid[dom * planes + p, b]
            for p in range(planes)
            for b in range(width)
        ]
        encode(
            rows,
            lambda index, value: out.__setitem__((dom, index), value),
            lambda value: out.__setitem__((dom, len(rows)), value),
        )
        return carry

    lax.fori_loop(0, dom_count, target, 0)


def nodal_rows(terms, slabs, dom_count):
    comp_count = terms.shape[0]
    width = GRID_B // dom_count
    chunks, _ = chunk_slices(comp_count, width)
    shape = (dom_count, (GRID_A // dom_count) * width + 1, GRID_C, LANES)
    return pl.pallas_call(
        lambda *refs: nodal_body(chunks, width, *refs),
        in_specs=[smem(), whole(terms.shape)],
        out_specs=whole(shape),
        grid=(1,),
        out_shape=jax.ShapeDtypeStruct(shape, jnp.int16),
        scratch_shapes=[pltpu.VMEM((GRID_A, width, GRID_C, LANES), jnp.float32)],
        compiler_params=params(),
    )(slabs, terms)


def final_body(weight, grid, change, out):
    planes, width = grid.shape[0], grid.shape[1]
    unit = unit_of(change[0, planes * width])
    for p in range(planes):
        for b in range(width):
            out[0, p, b] = grid[p, b] * weight[0] + to_float(change[0, p * width + b]) * unit


def final_planes(grid, change, weight):
    planes = grid.shape[0]
    dom_count = change.shape[0]
    width = GRID_B // dom_count
    return pl.pallas_call(
        final_body,
        grid=(dom_count,),
        in_specs=[
            smem(),
            pl.BlockSpec((planes, width, GRID_C, LANES), lambda e: (0, e, 0, 0)),
            pl.BlockSpec((1,) + change.shape[1:], lambda e: (e, 0, 0, 0)),
        ],
        out_specs=pl.BlockSpec((1, planes, width, GRID_C, LANES), lambda e: (0, 0, e, 0, 0)),
        out_shape=jax.ShapeDtypeStruct((1,) + grid.shape, jnp.float32),
        compiler_params=params(),
    )(weight, grid, change)


def merge_tables(owner_lists, comp_count):
    is_multi = jnp.sum((owner_lists >= 0).astype(jnp.int32), axis=1) > 1
    block = jnp.arange(owner_lists.shape[0], dtype=jnp.int32)
    earlier = (block[None, :] < block[:, None]) & is_multi[None, :]
    rank = jnp.sum(earlier.astype(jnp.int32), axis=1)
    mark = jnp.where(is_multi, rank + 1, 0)
    slab = jnp.arange(comp_count * GRID_A, dtype=jnp.int32)
    hits = owner_lists[None, :, :] == slab[:, None, None]
    marks = jnp.sum(jnp.where(hits, mark[None, :, None], 0), axis=(1, 2)).reshape(comp_count, GRID_A)
    first = jnp.arange(GRID_A, dtype=jnp.int32)
    before = (first[None, :] < first[:, None])[None] & (marks > 0)[:, None, :]
    place = jnp.sum(before.astype(jnp.int32), axis=2)
    chosen = (place[:, None, :] == jnp.arange(MULTI)[None, :, None]) & (marks > 0)[:, None, :]
    slabs = jnp.sum(jnp.where(chosen, first[None, None, :], 0), axis=2)
    blocks = jnp.sum(jnp.where(chosen, marks[:, None, :] - 1, 0), axis=2)
    return slabs, blocks


def local(density, velocity, coefficients, owner_lists):
    comp_count, dom_count = lax.axis_size("comp"), lax.axis_size("dom")
    comp_index = lax.axis_index("comp")
    upward = [(i, (i + 1) % dom_count) for i in range(dom_count)]
    downward = [(target, source) for source, target in upward]

    slabs, blocks = merge_tables(owner_lists, comp_count)
    own = lax.dynamic_index_in_dim(slabs, comp_index, 0, keepdims=False)
    spacing = own & -own
    own_slabs = jnp.stack([own, (own - spacing) % GRID_A, (own + spacing) % GRID_A])
    weight = lax.dynamic_slice_in_dim(coefficients, comp_index, 1).astype(jnp.float32)

    grid = density[0]
    first, last = send_planes(density)
    for step in range(STEPS):
        low = lax.ppermute(last, "dom", upward)
        high = lax.ppermute(first, "dom", downward)
        partial = inner_planes(grid, velocity)
        if step < STEPS - 1:
            grid, first, last = edge_planes(grid, low, high, velocity, partial, True)
        else:
            (grid,) = edge_planes(grid, low, high, velocity, partial, False)
    columns = lax.all_to_all(spread_columns(grid, dom_count), "dom", 0, 0, tiled=True)
    terms = surplus_rows(columns, own_slabs, weight, comp_count)
    terms = lax.all_to_all(terms, "comp", 0, 0, tiled=True)
    terms = merge_rows(terms, blocks)
    terms = lax.all_to_all(terms, "comp", 0, 0, tiled=True)
    change = nodal_rows(terms, own_slabs, dom_count)
    change = lax.all_to_all(change, "dom", 0, 0, tiled=True)
    return final_planes(grid, change, weight)


def solution(mesh):
    in_specs = (
        P("comp", "dom", None, None, None),
        P("comp", None, "dom", None, None, None),
        P(),
        P(),
    )
    out_specs = P("comp", "dom", None, None, None)
    return jax.shard_map(local, mesh=mesh, in_specs=in_specs, out_specs=out_specs, check_vma=False)
```

```python
import functools

import jax
import jax.numpy as jnp
import numpy as np
from jax import lax
from jax.experimental import pallas as pl
from jax.experimental.pallas import tpu as pltpu
from jax.sharding import PartitionSpec as P

GRID_A = 32
GRID_B = 16
GRID_C = 16
LANES = 256
HALF = 128
LANE_AXES = ((8, 32), (8, 4), (4, 1))
STEPS = 4
GROUP = 4
SHARED = 4
BORROWED = 4
MULTI = 12
LEVELS = 32000.0
FINE = 16.0
TINY = 1e-36
VMEM_LIMIT = 48 * 1024 * 1024


def params():
    return pltpu.CompilerParams(vmem_limit_bytes=VMEM_LIMIT)


def smem():
    return pl.BlockSpec(memory_space=pltpu.SMEM)


def whole(shape):
    return pl.BlockSpec(shape, lambda *_: (0,) * len(shape))


def code_of(peak):
    return jnp.ceil(jnp.log(jnp.maximum(peak, TINY)) * (FINE / 0.6931471805599453))


def encode(rows, put, put_code):
    peak = jnp.abs(rows[0]())
    for row in rows[1:]:
        peak = jnp.maximum(peak, jnp.abs(row()))
    code = code_of(peak)
    factor = jnp.exp2(code * (-1.0 / FINE)) * LEVELS
    put_code(code.astype(jnp.int32).astype(jnp.int16))
    for index, row in enumerate(rows):
        put(index, jnp.round(row() * factor).astype(jnp.int32).astype(jnp.int16))


def to_float(block):
    return block.astype(jnp.int32).astype(jnp.float32)


def unit_of(code_row):
    return jnp.exp2(to_float(code_row) * (1.0 / FINE)) * (1.0 / LEVELS)


def send_planes_body(first, last, out_first, out_last):
    for source, out in ((first, out_first), (last, out_last)):
        rows = [lambda b=b, source=source: source[0, 0, b] for b in range(GRID_B)]
        encode(
            rows,
            lambda b, value, out=out: out.__setitem__(b, value),
            lambda value, out=out: out.__setitem__(GRID_B, value),
        )


def message_shape():
    return jax.ShapeDtypeStruct((GRID_B + 1, GRID_C, LANES), jnp.int16)


def send_planes(density):
    planes = density.shape[1]
    block = (1, 1, GRID_B, GRID_C, LANES)
    return pl.pallas_call(
        send_planes_body,
        grid=(1,),
        in_specs=[
            pl.BlockSpec(block, lambda i: (0, 0, 0, 0, 0)),
            pl.BlockSpec(block, lambda i: (0, planes - 1, 0, 0, 0)),
        ],
        out_specs=[whole(message_shape().shape)] * 2,
        out_shape=[message_shape()] * 2,
        compiler_params=params(),
    )(density, density)


def lane_matrix():
    point = np.arange(LANES)
    eye = np.eye(LANES)
    total = np.zeros((LANES, LANES))
    differences = []
    for extent, stride in LANE_AXES:
        place = point // stride % extent
        forward = eye[:, point + ((place + 1) % extent - place) * stride]
        backward = eye[:, point + ((place - 1) % extent - place) * stride]
        total += forward + backward
        differences.append(forward - backward)
    matrix = np.concatenate([total] + differences, 1)
    return jnp.asarray(np.concatenate([matrix, matrix], 0), jnp.bfloat16)


def lane_products(plane, matrix, products):
    value = plane.reshape(GRID_B * GRID_C, LANES)
    coarse = value.astype(jnp.bfloat16)
    fine = (value - coarse.astype(jnp.float32)).astype(jnp.bfloat16)
    products[...] = jnp.dot(
        jnp.concatenate([coarse, fine], 1), matrix[...], preferred_element_type=jnp.float32
    )


def advance_row(b, value, above, below, plane_row, products, speeds):
    rates = [speeds[0, d, 0, b].astype(jnp.float32) for d in range(6)]
    pairs = [
        (above, below),
        (plane_row(lax.rem(b + 1, GRID_B)), plane_row(lax.rem(b + GRID_B - 1, GRID_B))),
        (pltpu.roll(value, GRID_C - 1, 0), pltpu.roll(value, 1, 0)),
    ]
    rows = pl.ds(pl.multiple_of(b * GRID_C, GRID_C), GRID_C)
    total = products[rows, :LANES]
    drift = None
    for index, rate in enumerate(rates):
        if index < 3:
            forward, backward = pairs[index]
            total = total + (forward + backward)
            difference = forward - backward
        else:
            difference = products[rows, (index - 2) * LANES : (index - 1) * LANES]
        term = rate * difference
        drift = term if drift is None else drift + term
    return 0.28 * value + 0.06 * total - 0.5 * drift


def inner_body(grid, matrix, speeds, out, products):
    plane = pl.program_id(0) + 1
    lane_products(grid[plane], matrix, products)

    def row(b, carry):
        out[0, b] = advance_row(
            b,
            grid[plane, b],
            grid[plane + 1, b],
            grid[plane - 1, b],
            lambda near: grid[plane, near],
            products,
            speeds,
        )
        return carry

    lax.fori_loop(0, GRID_B, row, 0, unroll=2)


def products_scratch():
    return pltpu.VMEM((GRID_B * GRID_C, 4 * LANES), jnp.float32)


def inner_planes(grid, matrix, velocity):
    planes = grid.shape[0]
    points = (planes - 2) * GRID_B * GRID_C * LANES
    return pl.pallas_call(
        inner_body,
        grid=(planes - 2,),
        in_specs=[
            whole(grid.shape),
            whole(matrix.shape),
            pl.BlockSpec((1, 6, 1, GRID_B, GRID_C, LANES), lambda p: (0, 0, p + 1, 0, 0, 0)),
        ],
        out_specs=pl.BlockSpec((1, GRID_B, GRID_C, LANES), lambda p: (p + 1, 0, 0, 0)),
        out_shape=jax.ShapeDtypeStruct(grid.shape, jnp.float32),
        scratch_shapes=[products_scratch()],
        compiler_params=params(),
        cost_estimate=pl.CostEstimate(
            flops=40 * points, bytes_accessed=20 * points, transcendentals=0
        ),
    )(grid, matrix, velocity)


def edge_body(message, mid, near, low, high, matrix, speeds, partial, out, *rest):
    del partial
    *messages, halo, products = rest
    side = pl.program_id(0)
    lane_products(mid[0], matrix, products)

    def unpack(source):
        unit = unit_of(source[GRID_B])
        for b in range(GRID_B):
            halo[b] = to_float(source[b]) * unit

    @pl.when(side == 0)
    def _():
        unpack(low)

    @pl.when(side == 1)
    def _():
        unpack(high)

    def row(b, carry):
        outer, inside = halo[b], near[0, b]
        out[0, b] = advance_row(
            b,
            mid[0, b],
            jnp.where(side == 0, inside, outer),
            jnp.where(side == 0, outer, inside),
            lambda other: mid[0, other],
            products,
            speeds,
        )
        return carry

    lax.fori_loop(0, GRID_B, row, 0, unroll=2)
    if message:
        rows = [lambda b=b: out[0, b] for b in range(GRID_B)]
        for which, target in enumerate(messages):

            @pl.when(side == which)
            def _(target=target):
                encode(
                    rows,
                    lambda b, value: target.__setitem__(b, value),
                    lambda value: target.__setitem__(GRID_B, value),
                )


def edge_planes(grid, low, high, matrix, velocity, partial, message):
    planes = grid.shape[0]
    plane = (1, GRID_B, GRID_C, LANES)
    points = 2 * GRID_B * GRID_C * LANES
    out_specs = [pl.BlockSpec(plane, lambda i: (i * (planes - 1), 0, 0, 0))]
    out_shape = [jax.ShapeDtypeStruct(grid.shape, jnp.float32)]
    if message:
        out_specs += [whole(message_shape().shape)] * 2
        out_shape += [message_shape()] * 2
    return pl.pallas_call(
        lambda *refs: edge_body(message, *refs),
        grid=(2,),
        in_specs=[
            pl.BlockSpec(plane, lambda i: (i * (planes - 1), 0, 0, 0)),
            pl.BlockSpec(plane, lambda i: (1 + i * (planes - 3), 0, 0, 0)),
            whole(message_shape().shape),
            whole(message_shape().shape),
            whole(matrix.shape),
            pl.BlockSpec(
                (1, 6, 1, GRID_B, GRID_C, LANES), lambda i: (0, 0, i * (planes - 1), 0, 0, 0)
            ),
            pl.BlockSpec(memory_space=pl.ANY),
        ],
        out_specs=out_specs,
        out_shape=out_shape,
        scratch_shapes=[pltpu.VMEM((GRID_B, GRID_C, LANES), jnp.float32), products_scratch()],
        input_output_aliases={6: 0},
        compiler_params=params(),
        cost_estimate=pl.CostEstimate(
            flops=50 * points, bytes_accessed=24 * points, transcendentals=0
        ),
    )(grid, grid, low, high, matrix, velocity, partial)


def chunk_slices(count):
    splits = count // (2 * GRID_B)
    extent = GRID_C // splits
    return [
        (b, slice(part * extent, (part + 1) * extent), slice(half * HALF, (half + 1) * HALF))
        for b in range(GRID_B)
        for half in range(2)
        for part in range(splits)
    ], extent


def group_of(chunks):
    return len(chunks) // GRID_B * GROUP


def spread_body(chunks, grid, out):
    planes = grid.shape[0]
    for which, (b, third, lanes) in enumerate(chunks):
        encode(
            [lambda p=p: grid[p, b, third, lanes] for p in range(planes)],
            lambda index, value: out.__setitem__((which, index), value),
            lambda value: out.__setitem__((which, planes), value),
        )


def spread_columns(grid, count):
    planes = grid.shape[0]
    chunks, extent = chunk_slices(count)
    shape = (count, planes + 1, extent, HALF)
    group = group_of(chunks)
    return pl.pallas_call(
        functools.partial(spread_body, chunks[:group]),
        grid=(GRID_B // GROUP,),
        in_specs=[pl.BlockSpec((planes, GROUP, GRID_C, LANES), lambda e: (0, e, 0, 0))],
        out_specs=pl.BlockSpec((group,) + shape[1:], lambda e: (e, 0, 0, 0)),
        out_shape=jax.ShapeDtypeStruct(shape, jnp.int16),
        compiler_params=params(),
    )(grid)


def merge_body(dom_count, slabs, blocks, weights, columns, out, sums, rows, grid):
    planes = GRID_A // dom_count
    comp_count = columns.shape[0] // dom_count

    sums[...] = jnp.zeros_like(sums)

    def gather(comp, carry):
        weight = weights[comp].astype(jnp.float32)
        for index in range(MULTI):
            slab = slabs[comp, index]
            spacing = slab & -slab
            share = jnp.where(slab > 0, -0.5 * weight, 0.0)
            total = None
            for place, factor in (
                (slab, weight),
                ((slab - spacing) & (GRID_A - 1), share),
                ((slab + spacing) & (GRID_A - 1), share),
            ):
                source = comp * dom_count + lax.div(place, planes)
                value = to_float(columns[source, lax.rem(place, planes)])
                term = value * (unit_of(columns[source, planes]) * factor)
                total = term if total is None else total + term
            rows[comp, index] = total
            block = blocks[comp, index]
            sums[block] = sums[block] + total
        return carry

    lax.fori_loop(0, comp_count, gather, 0)

    def scatter(comp, carry):
        grid[...] = jnp.zeros_like(grid)
        for index in range(MULTI):
            grid[slabs[comp, index]] = sums[blocks[comp, index]] - rows[comp, index]
        spacing = GRID_A // 2
        while spacing >= 1:
            for position in range(spacing, GRID_A, 2 * spacing):
                grid[position] = grid[position] + 0.5 * (
                    grid[position - spacing] + grid[(position + spacing) % GRID_A]
                )
            spacing //= 2
        for dom in range(dom_count):
            target = comp * dom_count + dom
            encode(
                [lambda p=p, dom=dom: grid[dom * planes + p] for p in range(planes)],
                lambda index, value: out.__setitem__((target, index), value),
                lambda value: out.__setitem__((target, planes), value),
            )
        return carry

    lax.fori_loop(0, comp_count, scatter, 0)


def merge_columns(columns, slabs, blocks, weights, dom_count):
    comp_count = columns.shape[0] // dom_count
    tile = columns.shape[2:]
    return pl.pallas_call(
        functools.partial(merge_body, dom_count),
        in_specs=[smem(), smem(), smem(), whole(columns.shape)],
        out_specs=whole(columns.shape),
        grid=(1,),
        out_shape=jax.ShapeDtypeStruct(columns.shape, jnp.int16),
        scratch_shapes=[
            pltpu.VMEM((SHARED + comp_count * BORROWED,) + tile, jnp.float32),
            pltpu.VMEM((comp_count, MULTI) + tile, jnp.float32),
            pltpu.VMEM((GRID_A,) + tile, jnp.float32),
        ],
        compiler_params=params(),
    )(slabs, blocks, weights, columns)


def final_body(chunks, weight, grid, change, out):
    planes = grid.shape[0]
    for which, (b, third, lanes) in enumerate(chunks):
        unit = unit_of(change[which, planes])
        for p in range(planes):
            out[0, p, b, third, lanes] = (
                grid[p, b, third, lanes] * weight[0] + to_float(change[which, p]) * unit
            )


def final_planes(grid, change, weight):
    planes = grid.shape[0]
    chunks, _ = chunk_slices(change.shape[0])
    group = group_of(chunks)
    return pl.pallas_call(
        functools.partial(final_body, chunks[:group]),
        grid=(GRID_B // GROUP,),
        in_specs=[
            smem(),
            pl.BlockSpec((planes, GROUP, GRID_C, LANES), lambda e: (0, e, 0, 0)),
            pl.BlockSpec((group,) + change.shape[1:], lambda e: (e, 0, 0, 0)),
        ],
        out_specs=pl.BlockSpec((1, planes, GROUP, GRID_C, LANES), lambda e: (0, 0, e, 0, 0)),
        out_shape=jax.ShapeDtypeStruct((1,) + grid.shape, jnp.float32),
        compiler_params=params(),
    )(weight, grid, change)


def merge_tables(owner_lists, comp_count):
    is_multi = jnp.sum((owner_lists >= 0).astype(jnp.int32), axis=1) > 1
    block = jnp.arange(owner_lists.shape[0], dtype=jnp.int32)
    earlier = (block[None, :] < block[:, None]) & is_multi[None, :]
    rank = jnp.sum(earlier.astype(jnp.int32), axis=1)
    mark = jnp.where(is_multi, rank + 1, 0)
    slab = jnp.arange(comp_count * GRID_A, dtype=jnp.int32)
    hits = owner_lists[None, :, :] == slab[:, None, None]
    marks = jnp.sum(jnp.where(hits, mark[None, :, None], 0), axis=(1, 2)).reshape(comp_count, GRID_A)
    first = jnp.arange(GRID_A, dtype=jnp.int32)
    before = (first[None, :] < first[:, None])[None] & (marks > 0)[:, None, :]
    place = jnp.sum(before.astype(jnp.int32), axis=2)
    chosen = (place[:, None, :] == jnp.arange(MULTI)[None, :, None]) & (marks > 0)[:, None, :]
    slabs = jnp.sum(jnp.where(chosen, first[None, None, :], 0), axis=2)
    blocks = jnp.sum(jnp.where(chosen, marks[:, None, :] - 1, 0), axis=2)
    return slabs, blocks


def local(density, velocity, coefficients, owner_lists):
    comp_count, dom_count = lax.axis_size("comp"), lax.axis_size("dom")
    comp_index = lax.axis_index("comp")
    upward = [(i, (i + 1) % dom_count) for i in range(dom_count)]
    downward = [(target, source) for source, target in upward]

    slabs, blocks = merge_tables(owner_lists, comp_count)
    weight = lax.dynamic_slice_in_dim(coefficients, comp_index, 1).astype(jnp.float32)
    matrix = lane_matrix()

    grid = density[0]
    first, last = send_planes(density)
    for step in range(STEPS):
        low = lax.ppermute(last, "dom", upward)
        high = lax.ppermute(first, "dom", downward)
        partial = inner_planes(grid, matrix, velocity)
        if step < STEPS - 1:
            grid, first, last = edge_planes(grid, low, high, matrix, velocity, partial, True)
        else:
            (grid,) = edge_planes(grid, low, high, matrix, velocity, partial, False)
    columns = spread_columns(grid, comp_count * dom_count)
    columns = lax.all_to_all(columns, ("comp", "dom"), 0, 0, tiled=True)
    change = merge_columns(columns, slabs, blocks, coefficients, dom_count)
    change = lax.all_to_all(change, ("comp", "dom"), 0, 0, tiled=True)
    return final_planes(grid, change, weight)


def solution(mesh):
    in_specs = (
        P("comp", "dom", None, None, None),
        P("comp", None, "dom", None, None, None),
        P(),
        P(),
    )
    out_specs = P("comp", "dom", None, None, None)
    return jax.shard_map(local, mesh=mesh, in_specs=in_specs, out_specs=out_specs, check_vma=False)
```

```python
import functools

import jax
import jax.numpy as jnp
import numpy as np
from jax import lax
from jax.experimental import pallas as pl
from jax.experimental.pallas import tpu as pltpu
from jax.sharding import PartitionSpec as P

GRID_A = 32
GRID_B = 16
GRID_C = 16
LANES = 256
HALF = 128
D_STRIDE = 32
LANE_AXES = ((8, 4), (4, 1))
STEPS = 4
GROUP = 4
SHARED = 4
BORROWED = 4
MULTI = 12
LEVELS = 32000.0
FINE = 16.0
TINY = 1e-36
VMEM_LIMIT = 24 * 1024 * 1024


def params():
    return pltpu.CompilerParams(vmem_limit_bytes=VMEM_LIMIT)


def smem():
    return pl.BlockSpec(memory_space=pltpu.SMEM)


def whole(shape):
    return pl.BlockSpec(shape, lambda *_: (0,) * len(shape))


def code_of(peak):
    return jnp.ceil(jnp.log(jnp.maximum(peak, TINY)) * (FINE / 0.6931471805599453))


def encode(rows, put, put_code):
    peak = jnp.abs(rows[0]())
    for row in rows[1:]:
        peak = jnp.maximum(peak, jnp.abs(row()))
    code = code_of(peak)
    factor = jnp.exp2(code * (-1.0 / FINE)) * LEVELS
    put_code(code.astype(jnp.int32).astype(jnp.int16))
    for index, row in enumerate(rows):
        put(index, jnp.round(row() * factor).astype(jnp.int32).astype(jnp.int16))


def to_float(block):
    return block.astype(jnp.int32).astype(jnp.float32)


def unit_of(code_row):
    return jnp.exp2(to_float(code_row) * (1.0 / FINE)) * (1.0 / LEVELS)


def message_shape():
    return jax.ShapeDtypeStruct((GRID_B + 1, GRID_C, LANES), jnp.int16)


def send_planes_body(grid, *messages):
    for plane, target in zip((0, grid.shape[0] - 1), messages):
        encode(
            [lambda b=b: grid[plane, b] for b in range(GRID_B)],
            lambda b, value: target.__setitem__(b, value),
            lambda value: target.__setitem__(GRID_B, value),
        )


def send_planes(grid):
    return pl.pallas_call(
        send_planes_body,
        in_specs=[vmem()],
        out_specs=[vmem()] * 2,
        out_shape=[message_shape()] * 2,
        compiler_params=params(),
    )(grid)


def lane_matrix():
    point = np.arange(LANES)
    eye = np.eye(LANES)
    total = np.zeros((LANES, LANES))
    differences = []
    for extent, stride in LANE_AXES:
        place = point // stride % extent
        forward = eye[:, point + ((place + 1) % extent - place) * stride]
        backward = eye[:, point + ((place - 1) % extent - place) * stride]
        total += forward + backward
        differences.append(forward - backward)
    matrix = np.concatenate([total] + differences, 1)
    return jnp.asarray(np.concatenate([matrix, matrix], 0), jnp.bfloat16)


def lane_products(plane, matrix, products):
    value = plane.reshape(GRID_B * GRID_C, LANES)
    coarse = value.astype(jnp.bfloat16)
    fine = (value - coarse.astype(jnp.float32)).astype(jnp.bfloat16)
    products[...] = jnp.dot(
        jnp.concatenate([coarse, fine], 1), matrix[...], preferred_element_type=jnp.float32
    )


def advance_body(grid, matrix, speeds, out, even, odd):
    planes = grid.shape[0]

    def rows(plane, products):
        up, down = jnp.minimum(plane + 1, planes - 1), jnp.maximum(plane - 1, 0)
        has_up = jnp.where(plane < planes - 1, 1.0, 0.0)
        has_down = jnp.where(plane > 0, 1.0, 0.0)
        for b in range(GRID_B):
            value = grid[plane, b]
            pairs = [
                (grid[up, b] * has_up, grid[down, b] * has_down),
                (grid[plane, (b + 1) % GRID_B], grid[plane, (b - 1) % GRID_B]),
                (pltpu.roll(value, GRID_C - 1, 0), pltpu.roll(value, 1, 0)),
                (pltpu.roll(value, LANES - D_STRIDE, 1), pltpu.roll(value, D_STRIDE, 1)),
            ]
            place = slice(b * GRID_C, (b + 1) * GRID_C)
            total = products[place, :LANES]
            drift = None
            for d in range(6):
                if d < len(pairs):
                    forward, backward = pairs[d]
                    total = total + (forward + backward)
                    difference = forward - backward
                else:
                    difference = products[place, (d - 3) * LANES : (d - 2) * LANES]
                term = speeds[0, d, plane, b].astype(jnp.float32) * difference
                drift = term if drift is None else drift + term
            out[plane, b] = 0.28 * value + 0.06 * total - 0.5 * drift

    lane_products(grid[0], matrix, even)

    def pair(index, carry):
        plane = 2 * index
        lane_products(grid[plane + 1], matrix, odd)
        rows(plane, even)
        lane_products(grid[jnp.minimum(plane + 2, planes - 1)], matrix, even)
        rows(plane + 1, odd)
        return carry

    lax.fori_loop(0, planes // 2, pair, 0)


def vmem():
    return pl.BlockSpec(memory_space=pltpu.VMEM)


def advance_planes(grid, matrix, velocity):
    points = grid.size
    products = pltpu.VMEM((GRID_B * GRID_C, matrix.shape[1]), jnp.float32)
    return pl.pallas_call(
        advance_body,
        in_specs=[vmem()] * 3,
        out_specs=vmem(),
        out_shape=jax.ShapeDtypeStruct(grid.shape, jnp.float32),
        scratch_shapes=[products, products],
        compiler_params=params(),
        cost_estimate=pl.CostEstimate(
            flops=1000 * points, bytes_accessed=20 * points, transcendentals=0
        ),
    )(grid, matrix, velocity)


def edge_body(partial, low, high, speeds, out, *messages):
    del partial
    planes = out.shape[0]
    for plane, source, sign in ((0, low, 0.5), (planes - 1, high, -0.5)):
        unit = unit_of(source[GRID_B])
        for b in range(GRID_B):
            share = 0.06 + sign * speeds[0, 0, plane, b].astype(jnp.float32)
            out[plane, b] = out[plane, b] + to_float(source[b]) * unit * share
    for plane, target in zip((0, planes - 1), messages):
        encode(
            [lambda b=b: out[plane, b] for b in range(GRID_B)],
            lambda b, value: target.__setitem__(b, value),
            lambda value: target.__setitem__(GRID_B, value),
        )


def edge_planes(partial, low, high, velocity, message):
    count = 2 if message else 0
    return pl.pallas_call(
        edge_body,
        in_specs=[vmem()] * 4,
        out_specs=[vmem()] * (1 + count),
        out_shape=[jax.ShapeDtypeStruct(partial.shape, jnp.float32)] + [message_shape()] * count,
        input_output_aliases={0: 0},
        compiler_params=params(),
        cost_estimate=pl.CostEstimate(
            flops=2_000_000, bytes_accessed=2_000_000, transcendentals=0
        ),
    )(partial, low, high, velocity)


def chunk_slices(count):
    splits = count // (2 * GRID_B)
    extent = GRID_C // splits
    return [
        (b, slice(part * extent, (part + 1) * extent), slice(half * HALF, (half + 1) * HALF))
        for b in range(GRID_B)
        for half in range(2)
        for part in range(splits)
    ], extent


def group_of(chunks):
    return len(chunks) // GRID_B * GROUP


def spread_body(chunks, grid, out):
    planes = grid.shape[0]
    for which, (b, third, lanes) in enumerate(chunks):
        encode(
            [lambda p=p: grid[p, b, third, lanes] for p in range(planes)],
            lambda index, value: out.__setitem__((which, index), value),
            lambda value: out.__setitem__((which, planes), value),
        )


def spread_columns(grid, count):
    planes = grid.shape[0]
    chunks, extent = chunk_slices(count)
    shape = (count, planes + 1, extent, HALF)
    group = group_of(chunks)
    return pl.pallas_call(
        functools.partial(spread_body, chunks[:group]),
        grid=(GRID_B // GROUP,),
        in_specs=[pl.BlockSpec((planes, GROUP, GRID_C, LANES), lambda e: (0, e, 0, 0))],
        out_specs=pl.BlockSpec((group,) + shape[1:], lambda e: (e, 0, 0, 0)),
        out_shape=jax.ShapeDtypeStruct(shape, jnp.int16),
        compiler_params=params(),
    )(grid)


def merge_body(dom_count, slabs, blocks, weights, columns, out, sums, rows, grid):
    planes = GRID_A // dom_count
    comp_count = columns.shape[0] // dom_count

    sums[...] = jnp.zeros_like(sums)

    def gather(comp, carry):
        weight = weights[comp].astype(jnp.float32)
        for index in range(MULTI):
            slab = slabs[comp, index]
            spacing = slab & -slab
            share = jnp.where(slab > 0, -0.5 * weight, 0.0)
            total = None
            for place, factor in (
                (slab, weight),
                ((slab - spacing) & (GRID_A - 1), share),
                ((slab + spacing) & (GRID_A - 1), share),
            ):
                source = comp * dom_count + lax.div(place, planes)
                value = to_float(columns[source, lax.rem(place, planes)])
                term = value * (unit_of(columns[source, planes]) * factor)
                total = term if total is None else total + term
            rows[comp, index] = total
            block = blocks[comp, index]
            sums[block] = sums[block] + total
        return carry

    lax.fori_loop(0, comp_count, gather, 0)

    def scatter(comp, carry):
        grid[...] = jnp.zeros_like(grid)
        for index in range(MULTI):
            grid[slabs[comp, index]] = sums[blocks[comp, index]] - rows[comp, index]
        spacing = GRID_A // 2
        while spacing >= 1:
            for position in range(spacing, GRID_A, 2 * spacing):
                grid[position] = grid[position] + 0.5 * (
                    grid[position - spacing] + grid[(position + spacing) % GRID_A]
                )
            spacing //= 2
        for dom in range(dom_count):
            target = comp * dom_count + dom
            encode(
                [lambda p=p, dom=dom: grid[dom * planes + p] for p in range(planes)],
                lambda index, value: out.__setitem__((target, index), value),
                lambda value: out.__setitem__((target, planes), value),
            )
        return carry

    lax.fori_loop(0, comp_count, scatter, 0)


def merge_columns(columns, slabs, blocks, weights, dom_count):
    comp_count = columns.shape[0] // dom_count
    tile = columns.shape[2:]
    return pl.pallas_call(
        functools.partial(merge_body, dom_count),
        in_specs=[smem(), smem(), smem(), whole(columns.shape)],
        out_specs=whole(columns.shape),
        grid=(1,),
        out_shape=jax.ShapeDtypeStruct(columns.shape, jnp.int16),
        scratch_shapes=[
            pltpu.VMEM((SHARED + comp_count * BORROWED,) + tile, jnp.float32),
            pltpu.VMEM((comp_count, MULTI) + tile, jnp.float32),
            pltpu.VMEM((GRID_A,) + tile, jnp.float32),
        ],
        compiler_params=params(),
    )(slabs, blocks, weights, columns)


def final_body(chunks, weight, grid, change, out):
    planes = grid.shape[0]
    for which, (b, third, lanes) in enumerate(chunks):
        unit = unit_of(change[which, planes])
        for p in range(planes):
            out[0, p, b, third, lanes] = (
                grid[p, b, third, lanes] * weight[0] + to_float(change[which, p]) * unit
            )


def final_planes(grid, change, weight):
    planes = grid.shape[0]
    chunks, _ = chunk_slices(change.shape[0])
    group = group_of(chunks)
    return pl.pallas_call(
        functools.partial(final_body, chunks[:group]),
        grid=(GRID_B // GROUP,),
        in_specs=[
            smem(),
            pl.BlockSpec((planes, GROUP, GRID_C, LANES), lambda e: (0, e, 0, 0)),
            pl.BlockSpec((group,) + change.shape[1:], lambda e: (e, 0, 0, 0)),
        ],
        out_specs=pl.BlockSpec((1, planes, GROUP, GRID_C, LANES), lambda e: (0, 0, e, 0, 0)),
        out_shape=jax.ShapeDtypeStruct((1,) + grid.shape, jnp.float32),
        compiler_params=params(),
    )(weight, grid, change)


def merge_tables(owner_lists, comp_count):
    is_multi = jnp.sum((owner_lists >= 0).astype(jnp.int32), axis=1) > 1
    block = jnp.arange(owner_lists.shape[0], dtype=jnp.int32)
    earlier = (block[None, :] < block[:, None]) & is_multi[None, :]
    rank = jnp.sum(earlier.astype(jnp.int32), axis=1)
    mark = jnp.where(is_multi, rank + 1, 0)
    slab = jnp.arange(comp_count * GRID_A, dtype=jnp.int32)
    hits = owner_lists[None, :, :] == slab[:, None, None]
    marks = jnp.sum(jnp.where(hits, mark[None, :, None], 0), axis=(1, 2)).reshape(comp_count, GRID_A)
    first = jnp.arange(GRID_A, dtype=jnp.int32)
    before = (first[None, :] < first[:, None])[None] & (marks > 0)[:, None, :]
    place = jnp.sum(before.astype(jnp.int32), axis=2)
    chosen = (place[:, None, :] == jnp.arange(MULTI)[None, :, None]) & (marks > 0)[:, None, :]
    slabs = jnp.sum(jnp.where(chosen, first[None, None, :], 0), axis=2)
    blocks = jnp.sum(jnp.where(chosen, marks[:, None, :] - 1, 0), axis=2)
    return slabs, blocks


def local(density, velocity, coefficients, owner_lists):
    comp_count, dom_count = lax.axis_size("comp"), lax.axis_size("dom")
    comp_index = lax.axis_index("comp")
    upward = [(i, (i + 1) % dom_count) for i in range(dom_count)]
    downward = [(target, source) for source, target in upward]

    slabs, blocks = merge_tables(owner_lists, comp_count)
    weight = lax.dynamic_slice_in_dim(coefficients, comp_index, 1).astype(jnp.float32)
    matrix = lane_matrix()

    grid = density[0]
    first, last = send_planes(grid)
    for step in range(STEPS):
        low = lax.ppermute(last, "dom", upward)
        high = lax.ppermute(first, "dom", downward)
        partial = advance_planes(grid, matrix, velocity)
        if step < STEPS - 1:
            grid, first, last = edge_planes(partial, low, high, velocity, True)
        else:
            (grid,) = edge_planes(partial, low, high, velocity, False)
    columns = spread_columns(grid, comp_count * dom_count)
    columns = lax.all_to_all(columns, ("comp", "dom"), 0, 0, tiled=True)
    change = merge_columns(columns, slabs, blocks, coefficients, dom_count)
    change = lax.all_to_all(change, ("comp", "dom"), 0, 0, tiled=True)
    return final_planes(grid, change, weight)


def solution(mesh):
    in_specs = (
        P("comp", "dom", None, None, None),
        P("comp", None, "dom", None, None, None),
        P(),
        P(),
    )
    out_specs = P("comp", "dom", None, None, None)
    return jax.shard_map(local, mesh=mesh, in_specs=in_specs, out_specs=out_specs, check_vma=False)
```

```python
import functools

import jax
import jax.numpy as jnp
import numpy as np
from jax import lax
from jax.experimental import pallas as pl
from jax.experimental.pallas import tpu as pltpu
from jax.sharding import PartitionSpec as P

GRID_A = 32
GRID_B = 16
GRID_C = 16
LANES = 256
HALF = 128
D_STRIDE = 32
LANE_AXES = ((8, 4), (4, 1))
STEPS = 4
GROUP = 4
SHARED = 4
BORROWED = 4
MULTI = 12
LEVELS = 32000.0
FINE = 16.0
TINY = 1e-36
VMEM_LIMIT = 24 * 1024 * 1024


def params():
    return pltpu.CompilerParams(vmem_limit_bytes=VMEM_LIMIT)


def smem():
    return pl.BlockSpec(memory_space=pltpu.SMEM)


def whole(shape):
    return pl.BlockSpec(shape, lambda *_: (0,) * len(shape))


def code_of(peak):
    return jnp.ceil(jnp.log(jnp.maximum(peak, TINY)) * (FINE / 0.6931471805599453))


def encode(rows, put, put_code):
    peak = jnp.abs(rows[0]())
    for row in rows[1:]:
        peak = jnp.maximum(peak, jnp.abs(row()))
    code = code_of(peak)
    factor = jnp.exp2(code * (-1.0 / FINE)) * LEVELS
    put_code(code.astype(jnp.int32).astype(jnp.int16))
    for index, row in enumerate(rows):
        put(index, jnp.round(row() * factor).astype(jnp.int32).astype(jnp.int16))


def to_float(block):
    return block.astype(jnp.int32).astype(jnp.float32)


def unit_of(code_row):
    return jnp.exp2(to_float(code_row) * (1.0 / FINE)) * (1.0 / LEVELS)


def message_shape():
    return jax.ShapeDtypeStruct((GRID_B + 1, GRID_C, LANES), jnp.int16)


def send_planes_body(grid, *messages):
    for plane, target in zip((0, grid.shape[0] - 1), messages):
        encode(
            [lambda b=b: grid[plane, b] for b in range(GRID_B)],
            lambda b, value: target.__setitem__(b, value),
            lambda value: target.__setitem__(GRID_B, value),
        )


def send_planes(grid):
    return pl.pallas_call(
        send_planes_body,
        in_specs=[vmem()],
        out_specs=[vmem()] * 2,
        out_shape=[message_shape()] * 2,
        compiler_params=params(),
    )(grid)


def lane_matrix():
    point = np.arange(LANES)
    eye = np.eye(LANES)
    total = np.zeros((LANES, LANES))
    differences = []
    for extent, stride in LANE_AXES:
        place = point // stride % extent
        forward = eye[:, point + ((place + 1) % extent - place) * stride]
        backward = eye[:, point + ((place - 1) % extent - place) * stride]
        total += forward + backward
        differences.append(forward - backward)
    matrix = np.concatenate([total] + differences, 1)
    return jnp.asarray(np.concatenate([matrix, matrix], 0), jnp.bfloat16)


def lane_products(plane, matrix, products):
    value = plane.reshape(GRID_B * GRID_C, LANES)
    coarse = value.astype(jnp.bfloat16)
    fine = (value - coarse.astype(jnp.float32)).astype(jnp.bfloat16)
    products[...] = jnp.dot(
        jnp.concatenate([coarse, fine], 1), matrix[...], preferred_element_type=jnp.float32
    )


def advance_body(grid, matrix, speeds, out, even, odd):
    planes = grid.shape[0]

    def rows(plane, products):
        up, down = jnp.minimum(plane + 1, planes - 1), jnp.maximum(plane - 1, 0)
        has_up = jnp.where(plane < planes - 1, 1.0, 0.0)
        has_down = jnp.where(plane > 0, 1.0, 0.0)
        for b in range(GRID_B):
            value = grid[plane, b]
            pairs = [
                (grid[up, b] * has_up, grid[down, b] * has_down),
                (grid[plane, (b + 1) % GRID_B], grid[plane, (b - 1) % GRID_B]),
                (pltpu.roll(value, GRID_C - 1, 0), pltpu.roll(value, 1, 0)),
                (pltpu.roll(value, LANES - D_STRIDE, 1), pltpu.roll(value, D_STRIDE, 1)),
            ]
            place = slice(b * GRID_C, (b + 1) * GRID_C)
            total = products[place, :LANES]
            drift = None
            for d in range(6):
                if d < len(pairs):
                    forward, backward = pairs[d]
                    total = total + (forward + backward)
                    difference = forward - backward
                else:
                    difference = products[place, (d - 3) * LANES : (d - 2) * LANES]
                term = speeds[0, d, plane, b].astype(jnp.float32) * difference
                drift = term if drift is None else drift + term
            out[plane, b] = 0.28 * value + 0.06 * total - 0.5 * drift

    lane_products(grid[0], matrix, even)

    def pair(index, carry):
        plane = 2 * index
        lane_products(grid[plane + 1], matrix, odd)
        rows(plane, even)
        lane_products(grid[jnp.minimum(plane + 2, planes - 1)], matrix, even)
        rows(plane + 1, odd)
        return carry

    lax.fori_loop(0, planes // 2, pair, 0)


def vmem():
    return pl.BlockSpec(memory_space=pltpu.VMEM)


def advance_planes(grid, matrix, velocity):
    points = grid.size
    products = pltpu.VMEM((GRID_B * GRID_C, matrix.shape[1]), jnp.float32)
    return pl.pallas_call(
        advance_body,
        in_specs=[vmem()] * 3,
        out_specs=vmem(),
        out_shape=jax.ShapeDtypeStruct(grid.shape, jnp.float32),
        scratch_shapes=[products, products],
        compiler_params=params(),
        cost_estimate=pl.CostEstimate(
            flops=1000 * points, bytes_accessed=20 * points, transcendentals=0
        ),
    )(grid, matrix, velocity)


def add_edges(partial, low, high, speeds, out):
    del partial
    planes = out.shape[0]
    for plane, source, sign in ((0, low, 0.5), (planes - 1, high, -0.5)):
        unit = unit_of(source[GRID_B])
        for b in range(GRID_B):
            share = 0.06 + sign * speeds[0, 0, plane, b].astype(jnp.float32)
            out[plane, b] = out[plane, b] + to_float(source[b]) * unit * share


def edge_body(partial, low, high, speeds, out, *messages):
    add_edges(partial, low, high, speeds, out)
    for plane, target in zip((0, out.shape[0] - 1), messages):
        encode(
            [lambda b=b: out[plane, b] for b in range(GRID_B)],
            lambda b, value: target.__setitem__(b, value),
            lambda value: target.__setitem__(GRID_B, value),
        )


def edge_planes(partial, low, high, velocity):
    return pl.pallas_call(
        edge_body,
        in_specs=[vmem()] * 4,
        out_specs=[vmem()] * 3,
        out_shape=[jax.ShapeDtypeStruct(partial.shape, jnp.float32)] + [message_shape()] * 2,
        input_output_aliases={0: 0},
        compiler_params=params(),
        cost_estimate=pl.CostEstimate(
            flops=2_000_000, bytes_accessed=2_000_000, transcendentals=0
        ),
    )(partial, low, high, velocity)


class Cut:
    def __init__(self, count, planes):
        self.count, self.planes = count, planes
        self.splits = count // (2 * GRID_B)
        extent = GRID_C // self.splits
        self.pieces = 2 if extent == GRID_C else 1
        self.extent = extent // self.pieces
        self.stack = min(planes, max(1, 16 // self.extent))
        self.per_row = 2 * self.splits

    def rows(self, coded):
        return (self.planes + (1 if coded else 0)) * self.extent

    def shape(self, coded):
        return jax.ShapeDtypeStruct((self.count, self.rows(coded), HALF), jnp.int16)

    def places(self, chunk, piece):
        half, part = divmod(chunk, self.splits)
        start = (part * self.pieces + piece) * self.extent
        return slice(start, start + self.extent), slice(half * HALF, (half + 1) * HALF)

    def put(self, target, chunk, value_of, factor):
        size = self.stack * self.extent
        for index in range(0, self.planes, self.stack):
            block = jnp.concatenate(
                [value_of(index + i) * factor for i in range(self.stack)], 0
            )
            start = index * self.extent
            target[chunk, start : start + size] = (
                jnp.round(block).astype(jnp.int32).astype(jnp.int16)
            )

    def put_code(self, target, chunk, code):
        target[chunk, self.planes * self.extent :] = code.astype(jnp.int32).astype(jnp.int16)

    def code(self, source, chunk):
        return source[chunk, self.planes * self.extent :]

    def values(self, source, chunk, unit):
        values = []
        size = self.stack * self.extent
        for index in range(0, self.planes, self.stack):
            start = index * self.extent
            block = to_float(source[chunk, start : start + size])
            for i in range(self.stack):
                values.append(block[i * self.extent : (i + 1) * self.extent] * unit)
        return values


def factor_of(code):
    return jnp.exp2(code * (-1.0 / FINE)) * LEVELS


def peak_of(values):
    peak = jnp.abs(values[0])
    for value in values[1:]:
        peak = jnp.maximum(peak, jnp.abs(value))
    return peak


def last_body(cut, partial, low, high, speeds, grid, *rest):
    outs, stages, sems = rest[: cut.pieces], rest[cut.pieces : 2 * cut.pieces], rest[-1]
    add_edges(partial, low, high, speeds, grid)
    group = GROUP * cut.per_row

    def copy(index, piece):
        span = pl.ds(index * group, group)
        return pltpu.make_async_copy(
            stages[piece].at[span], outs[piece].at[span], sems.at[index, piece]
        )

    def pack(index, carry):
        for row in range(GROUP):
            b = index * GROUP + row
            for chunk in range(cut.per_row):
                places = [cut.places(chunk, piece) for piece in range(cut.pieces)]
                code = code_of(
                    peak_of([grid[(p, b) + place] for p in range(cut.planes) for place in places])
                )
                factor = factor_of(code)
                which = b * cut.per_row + chunk
                for piece, place in enumerate(places):
                    cut.put(
                        stages[piece], which, lambda p, place=place: grid[(p, b) + place], factor
                    )
                cut.put_code(stages[0], which, code)
        for piece in range(cut.pieces):
            copy(index, piece).start()
        return carry

    lax.fori_loop(0, GRID_B // GROUP, pack, 0)
    for index in range(GRID_B // GROUP):
        for piece in range(cut.pieces):
            copy(index, piece).wait()


def last_planes(cut, partial, low, high, velocity):
    shapes = [cut.shape(piece == 0) for piece in range(cut.pieces)]
    grid, *columns = pl.pallas_call(
        functools.partial(last_body, cut),
        in_specs=[vmem()] * 4,
        out_specs=[vmem()] + [pl.BlockSpec(memory_space=pltpu.HBM)] * cut.pieces,
        out_shape=[jax.ShapeDtypeStruct(partial.shape, jnp.float32)] + shapes,
        input_output_aliases={0: 0},
        scratch_shapes=[pltpu.VMEM(shape.shape, shape.dtype) for shape in shapes]
        + [pltpu.SemaphoreType.DMA((GRID_B // GROUP, cut.pieces))],
        compiler_params=params(),
    )(partial, low, high, velocity)
    return grid, columns


def merge_body(cut, dom_count, slabs, blocks, weights, codes, columns, out, values, sums, rows, grid):
    comp_count = cut.count // dom_count
    sums[...] = jnp.zeros_like(sums)

    def unpack(source, carry):
        unit = unit_of(cut.code(codes, source))
        for plane, value in enumerate(cut.values(columns, source, unit)):
            values[source * cut.planes + plane] = value
        return carry

    lax.fori_loop(0, cut.count, unpack, 0, unroll=2)

    def gather(comp, carry):
        weight = weights[comp].astype(jnp.float32)
        base = comp * GRID_A
        grid[comp] = jnp.zeros(grid.shape[1:], jnp.float32)
        for index in range(MULTI):
            slab = slabs[comp, index]
            spacing = slab & -slab
            share = jnp.where(slab > 0, -0.5 * weight, 0.0)
            near = (
                values[base + ((slab - spacing) & (GRID_A - 1))]
                + values[base + ((slab + spacing) & (GRID_A - 1))]
            )
            total = values[base + slab] * weight + near * share
            rows[comp, index] = total
            block = blocks[comp, index]
            sums[block] = sums[block] + total
        return carry

    lax.fori_loop(0, comp_count, gather, 0)

    def scatter(comp, carry):
        for index in range(MULTI):
            grid[comp, slabs[comp, index]] = sums[blocks[comp, index]] - rows[comp, index]
        nodal = [grid[comp, position] for position in range(GRID_A)]
        spacing = GRID_A // 2
        while spacing >= 1:
            for position in range(spacing, GRID_A, 2 * spacing):
                nodal[position] = nodal[position] + 0.5 * (
                    nodal[position - spacing] + nodal[(position + spacing) % GRID_A]
                )
            spacing //= 2
        for dom in range(dom_count):
            target = comp * dom_count + dom
            own = nodal[dom * cut.planes : (dom + 1) * cut.planes]
            code = code_of(peak_of(own))
            cut.put(out, target, lambda p, own=own: own[p], factor_of(code))
            cut.put_code(out, target, code)
        return carry

    lax.fori_loop(0, comp_count, scatter, 0)


def merge_columns(cut, columns, codes, slabs, blocks, weights, dom_count):
    comp_count = cut.count // dom_count
    tile = (cut.extent, HALF)
    points = cut.count * cut.planes * cut.extent * HALF
    return pl.pallas_call(
        functools.partial(merge_body, cut, dom_count),
        in_specs=[smem()] * 3 + [vmem()] * 2,
        out_specs=vmem(),
        out_shape=cut.shape(True),
        scratch_shapes=[
            pltpu.VMEM((comp_count * GRID_A,) + tile, jnp.float32),
            pltpu.VMEM((SHARED + comp_count * BORROWED,) + tile, jnp.float32),
            pltpu.VMEM((comp_count, MULTI) + tile, jnp.float32),
            pltpu.VMEM((comp_count, GRID_A) + tile, jnp.float32),
        ],
        compiler_params=params(),
        cost_estimate=pl.CostEstimate(
            flops=40 * points, bytes_accessed=8 * points, transcendentals=0
        ),
    )(slabs, blocks, weights, codes, columns)


def final_body(cut, weight, grid, *rest):
    *changes, out = rest
    for row in range(GROUP):
        for chunk in range(cut.per_row):
            which = row * cut.per_row + chunk
            for piece, change in enumerate(changes):
                place = cut.places(chunk, piece)
                unit = unit_of(cut.code(change, which))
                for p, value in enumerate(cut.values(change, which, unit)):
                    out[(0, p, row) + place] = grid[(p, row) + place] * weight[0] + value


def final_planes(cut, grid, changes, weight):
    group = GROUP * cut.per_row
    return pl.pallas_call(
        functools.partial(final_body, cut),
        grid=(GRID_B // GROUP,),
        in_specs=[
            smem(),
            pl.BlockSpec((cut.planes, GROUP, GRID_C, LANES), lambda e: (0, e, 0, 0)),
        ]
        + [pl.BlockSpec((group,) + change.shape[1:], lambda e: (e, 0, 0)) for change in changes],
        out_specs=pl.BlockSpec((1, cut.planes, GROUP, GRID_C, LANES), lambda e: (0, 0, e, 0, 0)),
        out_shape=jax.ShapeDtypeStruct((1,) + grid.shape, jnp.float32),
        compiler_params=params(),
    )(weight, grid, *changes)


def merge_tables(owner_lists, comp_count):
    is_multi = jnp.sum((owner_lists >= 0).astype(jnp.int32), axis=1) > 1
    block = jnp.arange(owner_lists.shape[0], dtype=jnp.int32)
    earlier = (block[None, :] < block[:, None]) & is_multi[None, :]
    rank = jnp.sum(earlier.astype(jnp.int32), axis=1)
    mark = jnp.where(is_multi, rank + 1, 0)
    slab = jnp.arange(comp_count * GRID_A, dtype=jnp.int32)
    hits = owner_lists[None, :, :] == slab[:, None, None]
    marks = jnp.sum(jnp.where(hits, mark[None, :, None], 0), axis=(1, 2)).reshape(comp_count, GRID_A)
    first = jnp.arange(GRID_A, dtype=jnp.int32)
    before = (first[None, :] < first[:, None])[None] & (marks > 0)[:, None, :]
    place = jnp.sum(before.astype(jnp.int32), axis=2)
    chosen = (place[:, None, :] == jnp.arange(MULTI)[None, :, None]) & (marks > 0)[:, None, :]
    slabs = jnp.sum(jnp.where(chosen, first[None, None, :], 0), axis=2)
    blocks = jnp.sum(jnp.where(chosen, marks[:, None, :] - 1, 0), axis=2)
    return slabs, blocks


def local(density, velocity, coefficients, owner_lists):
    comp_count, dom_count = lax.axis_size("comp"), lax.axis_size("dom")
    comp_index = lax.axis_index("comp")
    upward = [(i, (i + 1) % dom_count) for i in range(dom_count)]
    downward = [(target, source) for source, target in upward]

    slabs, blocks = merge_tables(owner_lists, comp_count)
    weight = lax.dynamic_slice_in_dim(coefficients, comp_index, 1).astype(jnp.float32)
    matrix = lane_matrix()

    grid = density[0]
    first, last = send_planes(grid)
    for step in range(STEPS):
        low = lax.ppermute(last, "dom", upward)
        high = lax.ppermute(first, "dom", downward)
        partial = advance_planes(grid, matrix, velocity)
        if step < STEPS - 1:
            grid, first, last = edge_planes(partial, low, high, velocity)
    cut = Cut(comp_count * dom_count, grid.shape[0])
    grid, columns = last_planes(cut, partial, low, high, velocity)
    columns = [lax.all_to_all(piece, ("comp", "dom"), 0, 0, tiled=True) for piece in columns]
    changes = []
    for piece in columns:
        change = merge_columns(cut, piece, columns[0], slabs, blocks, coefficients, dom_count)
        changes.append(lax.all_to_all(change, ("comp", "dom"), 0, 0, tiled=True))
    return final_planes(cut, grid, changes, weight)


def solution(mesh):
    in_specs = (
        P("comp", "dom", None, None, None),
        P("comp", None, "dom", None, None, None),
        P(),
        P(),
    )
    out_specs = P("comp", "dom", None, None, None)
    return jax.shard_map(local, mesh=mesh, in_specs=in_specs, out_specs=out_specs, check_vma=False)
```

```python
import functools

import jax
import jax.numpy as jnp
import numpy as np
from jax import lax
from jax.experimental import pallas as pl
from jax.experimental.pallas import tpu as pltpu
from jax.sharding import PartitionSpec as P

GRID_A = 32
GRID_B = 16
GRID_C = 16
LANES = 256
HALF = 128
D_STRIDE = 32
LANE_AXES = ((8, 4), (4, 1))
STEPS = 4
GROUP = 4
SHARED = 4
BORROWED = 4
MULTI = 12
LEVELS = 32000.0
FINE = 16.0
TINY = 1e-36
VMEM_LIMIT = 24 * 1024 * 1024
FIRST_LIMIT = 40 * 1024 * 1024
SEND_LIMIT = 60 * 1024 * 1024


def params(limit=VMEM_LIMIT):
    return pltpu.CompilerParams(vmem_limit_bytes=limit)


def smem():
    return pl.BlockSpec(memory_space=pltpu.SMEM)


def hbm():
    return pl.BlockSpec(memory_space=pltpu.HBM)


def vmem():
    return pl.BlockSpec(memory_space=pltpu.VMEM)


def code_of(peak):
    return jnp.ceil(jnp.log(jnp.maximum(peak, TINY)) * (FINE / 0.6931471805599453))


def encode(rows, put, put_code):
    peak = jnp.abs(rows[0]())
    for row in rows[1:]:
        peak = jnp.maximum(peak, jnp.abs(row()))
    code = code_of(peak)
    factor = jnp.exp2(code * (-1.0 / FINE)) * LEVELS
    put_code(code.astype(jnp.int32).astype(jnp.int16))
    for index, row in enumerate(rows):
        put(index, jnp.round(row() * factor).astype(jnp.int32).astype(jnp.int16))


def to_float(block):
    return block.astype(jnp.int32).astype(jnp.float32)


def unit_of(code_row):
    return jnp.exp2(to_float(code_row) * (1.0 / FINE)) * (1.0 / LEVELS)


def message_shape():
    return jax.ShapeDtypeStruct((GRID_B + 1, GRID_C, LANES), jnp.int16)


def send_planes_body(density, *rest):
    *messages, edges, sems = rest
    last = density.shape[1] - 1
    copies = [
        pltpu.make_async_copy(density.at[0, plane], edges.at[index], sems.at[index])
        for index, plane in enumerate((0, last))
    ]
    for copy in copies:
        copy.start()
    for index, target in enumerate(messages):
        copies[index].wait()
        encode(
            [lambda b=b: edges[index, b] for b in range(GRID_B)],
            lambda b, value: target.__setitem__(b, value),
            lambda value: target.__setitem__(GRID_B, value),
        )


def send_planes(density):
    return pl.pallas_call(
        send_planes_body,
        in_specs=[hbm()],
        out_specs=[vmem()] * 2,
        out_shape=[message_shape()] * 2,
        scratch_shapes=[
            pltpu.VMEM((2, GRID_B, GRID_C, LANES), jnp.float32),
            pltpu.SemaphoreType.DMA((2,)),
        ],
        compiler_params=params(SEND_LIMIT),
    )(density)


def lane_matrix():
    point = np.arange(LANES)
    eye = np.eye(LANES)
    total = np.zeros((LANES, LANES))
    differences = []
    for extent, stride in LANE_AXES:
        place = point // stride % extent
        forward = eye[:, point + ((place + 1) % extent - place) * stride]
        backward = eye[:, point + ((place - 1) % extent - place) * stride]
        total += forward + backward
        differences.append(forward - backward)
    matrix = np.concatenate([total] + differences, 1)
    return jnp.asarray(np.concatenate([matrix, matrix], 0), jnp.bfloat16)


def lane_products(plane, matrix, products):
    value = plane.reshape(GRID_B * GRID_C, LANES)
    coarse = value.astype(jnp.bfloat16)
    fine = (value - coarse.astype(jnp.float32)).astype(jnp.bfloat16)
    products[...] = jnp.dot(
        jnp.concatenate([coarse, fine], 1), matrix[...], preferred_element_type=jnp.float32
    )


def advance(grid, matrix, speeds, out, even, odd, ready):
    planes = grid.shape[0]

    def rows(plane, products):
        up, down = jnp.minimum(plane + 1, planes - 1), jnp.maximum(plane - 1, 0)
        has_up = jnp.where(plane < planes - 1, 1.0, 0.0)
        has_down = jnp.where(plane > 0, 1.0, 0.0)
        for b in range(GRID_B):
            value = grid[plane, b]
            pairs = [
                (grid[up, b] * has_up, grid[down, b] * has_down),
                (grid[plane, (b + 1) % GRID_B], grid[plane, (b - 1) % GRID_B]),
                (pltpu.roll(value, GRID_C - 1, 0), pltpu.roll(value, 1, 0)),
                (pltpu.roll(value, LANES - D_STRIDE, 1), pltpu.roll(value, D_STRIDE, 1)),
            ]
            place = slice(b * GRID_C, (b + 1) * GRID_C)
            total = products[place, :LANES]
            drift = None
            for d in range(6):
                if d < len(pairs):
                    forward, backward = pairs[d]
                    total = total + (forward + backward)
                    difference = forward - backward
                else:
                    difference = products[place, (d - 3) * LANES : (d - 2) * LANES]
                term = speeds[d, plane, b].astype(jnp.float32) * difference
                drift = term if drift is None else drift + term
            out[plane, b] = 0.28 * value + 0.06 * total - 0.5 * drift

    lane_products(grid[0], matrix, even)

    def pair(index, carry):
        plane = 2 * index
        ready(plane)
        lane_products(grid[plane + 1], matrix, odd)
        rows(plane, even)
        ready(plane + 1)
        lane_products(grid[jnp.minimum(plane + 2, planes - 1)], matrix, even)
        rows(plane + 1, odd)
        return carry

    lax.fori_loop(0, planes // 2, pair, 0)


def advance_body(grid, matrix, speeds, out, even, odd):
    advance(grid, matrix, speeds, out, even, odd, lambda plane: None)


def first_body(density, matrix, velocity, out, speeds, grid, even, odd, grid_sems, speed_sems):
    planes = grid.shape[0]

    def grid_copy(plane):
        return pltpu.make_async_copy(density.at[0, plane], grid.at[plane], grid_sems.at[plane])

    def speed_copy(plane):
        return pltpu.make_async_copy(
            velocity.at[0, :, plane], speeds.at[:, plane], speed_sems.at[plane]
        )

    for plane in range(planes):
        grid_copy(plane).start()
    for plane in range(planes):
        speed_copy(plane).start()
    for plane in range(planes):
        grid_copy(plane).wait()
    advance(grid, matrix, speeds, out, even, odd, lambda plane: speed_copy(plane).wait())


def first_planes(density, matrix, velocity):
    products = pltpu.VMEM((GRID_B * GRID_C, matrix.shape[1]), jnp.float32)
    planes = density.shape[1]
    return pl.pallas_call(
        first_body,
        in_specs=[hbm(), vmem(), hbm()],
        out_specs=[vmem()] * 2,
        out_shape=[
            jax.ShapeDtypeStruct(density.shape[1:], jnp.float32),
            jax.ShapeDtypeStruct(velocity.shape[1:], jnp.bfloat16),
        ],
        scratch_shapes=[
            pltpu.VMEM(density.shape[1:], jnp.float32),
            products,
            products,
            pltpu.SemaphoreType.DMA((planes,)),
            pltpu.SemaphoreType.DMA((planes,)),
        ],
        compiler_params=params(FIRST_LIMIT),
        cost_estimate=pl.CostEstimate(
            flops=1000 * density.size, bytes_accessed=20 * density.size, transcendentals=0
        ),
    )(density, matrix, velocity)


def advance_planes(grid, matrix, velocity):
    points = grid.size
    products = pltpu.VMEM((GRID_B * GRID_C, matrix.shape[1]), jnp.float32)
    return pl.pallas_call(
        advance_body,
        in_specs=[vmem()] * 3,
        out_specs=vmem(),
        out_shape=jax.ShapeDtypeStruct(grid.shape, jnp.float32),
        scratch_shapes=[products, products],
        compiler_params=params(),
        cost_estimate=pl.CostEstimate(
            flops=1000 * points, bytes_accessed=20 * points, transcendentals=0
        ),
    )(grid, matrix, velocity)


def add_edges(partial, low, high, speeds, out):
    del partial
    planes = out.shape[0]
    for plane, source, sign in ((0, low, 0.5), (planes - 1, high, -0.5)):
        unit = unit_of(source[GRID_B])
        for b in range(GRID_B):
            share = 0.06 + sign * speeds[0, plane, b].astype(jnp.float32)
            out[plane, b] = out[plane, b] + to_float(source[b]) * unit * share


def edge_body(partial, low, high, speeds, out, *messages):
    add_edges(partial, low, high, speeds, out)
    for plane, target in zip((0, out.shape[0] - 1), messages):
        encode(
            [lambda b=b: out[plane, b] for b in range(GRID_B)],
            lambda b, value: target.__setitem__(b, value),
            lambda value: target.__setitem__(GRID_B, value),
        )


def edge_planes(partial, low, high, velocity):
    return pl.pallas_call(
        edge_body,
        in_specs=[vmem()] * 4,
        out_specs=[vmem()] * 3,
        out_shape=[jax.ShapeDtypeStruct(partial.shape, jnp.float32)] + [message_shape()] * 2,
        input_output_aliases={0: 0},
        compiler_params=params(),
        cost_estimate=pl.CostEstimate(
            flops=2_000_000, bytes_accessed=2_000_000, transcendentals=0
        ),
    )(partial, low, high, velocity)


class Cut:
    def __init__(self, count, planes):
        self.count, self.planes = count, planes
        self.splits = count // (2 * GRID_B)
        self.extent = GRID_C // self.splits
        self.code_rows = min(self.extent, 8)
        self.groups = self.extent // self.code_rows
        self.data_rows = planes * self.extent
        self.stack = min(planes, max(1, 16 // self.extent))
        self.per_row = 2 * self.splits

    def shape(self):
        return jax.ShapeDtypeStruct(
            (self.count, self.data_rows + self.code_rows, HALF), jnp.int16
        )

    def place(self, chunk):
        half, part = divmod(chunk, self.splits)
        return (
            slice(part * self.extent, (part + 1) * self.extent),
            slice(half * HALF, (half + 1) * HALF),
        )

    def spread(self, tile, repeats=1):
        return jnp.concatenate([tile] * (self.groups * repeats), 0)

    def put(self, target, chunk, value_of):
        peak = jnp.abs(value_of(0))
        for plane in range(1, self.planes):
            peak = jnp.maximum(peak, jnp.abs(value_of(plane)))
        top = peak[: self.code_rows]
        for group in range(1, self.groups):
            top = jnp.maximum(top, peak[group * self.code_rows : (group + 1) * self.code_rows])
        code = code_of(top)
        factor = self.spread(jnp.exp2(code * (-1.0 / FINE)) * LEVELS, self.stack)
        size = self.stack * self.extent
        for index in range(0, self.planes, self.stack):
            block = jnp.concatenate([value_of(index + i) for i in range(self.stack)], 0)
            start = index * self.extent
            target[chunk, start : start + size] = (
                jnp.round(block * factor).astype(jnp.int32).astype(jnp.int16)
            )
        target[chunk, self.data_rows :] = code.astype(jnp.int32).astype(jnp.int16)

    def values(self, source, chunk):
        unit = self.spread(unit_of(source[chunk, self.data_rows :]), self.stack)
        values = []
        size = self.stack * self.extent
        for index in range(0, self.planes, self.stack):
            start = index * self.extent
            block = to_float(source[chunk, start : start + size]) * unit
            for i in range(self.stack):
                values.append(block[i * self.extent : (i + 1) * self.extent])
        return values


def last_body(cut, partial, low, high, speeds, grid, out):
    add_edges(partial, low, high, speeds, grid)

    def pack(index, carry):
        for row in range(GROUP):
            b = index * GROUP + row
            for chunk in range(cut.per_row):
                place = cut.place(chunk)
                cut.put(out, b * cut.per_row + chunk, lambda p: grid[(p, b) + place])
        return carry

    lax.fori_loop(0, GRID_B // GROUP, pack, 0)


def last_planes(cut, partial, low, high, velocity):
    return pl.pallas_call(
        functools.partial(last_body, cut),
        in_specs=[vmem()] * 4,
        out_specs=[vmem()] * 2,
        out_shape=[jax.ShapeDtypeStruct(partial.shape, jnp.float32), cut.shape()],
        input_output_aliases={0: 0},
        compiler_params=params(),
    )(partial, low, high, velocity)


def merge_body(cut, dom_count, slabs, partners, weights, columns, out, values, rows, sums, grid):
    comp_count = cut.count // dom_count

    def unpack(source, carry):
        for plane, value in enumerate(cut.values(columns, source)):
            values[source * cut.planes + plane] = value
        return carry

    lax.fori_loop(0, cut.count, unpack, 0, unroll=2)

    def gather(comp, carry):
        weight = weights[comp].astype(jnp.float32)
        base = comp * GRID_A
        for index in range(MULTI):
            slab = slabs[comp, index]
            spacing = slab & -slab
            share = jnp.where(slab > 0, -0.5 * weight, 0.0)
            near = (
                values[base + ((slab - spacing) & (GRID_A - 1))]
                + values[base + ((slab + spacing) & (GRID_A - 1))]
            )
            rows[comp * MULTI + index] = values[base + slab] * weight + near * share
        return carry

    lax.fori_loop(0, comp_count, gather, 0)
    for index in range(SHARED):
        total = rows[index]
        for comp in range(1, comp_count):
            total = total + rows[comp * MULTI + index]
        sums[index] = total
    grid[...] = jnp.zeros_like(grid)

    def scatter(comp, carry):
        for index in range(MULTI):
            if index < SHARED:
                change = sums[index] - rows[comp * MULTI + index]
            else:
                change = rows[partners[comp, index]]
            grid[comp, slabs[comp, index]] = change
        return carry

    lax.fori_loop(0, comp_count, scatter, 0)

    def send(comp, carry):
        nodal = [grid[comp, position] for position in range(GRID_A)]
        spacing = GRID_A // 2
        while spacing >= 1:
            for position in range(spacing, GRID_A, 2 * spacing):
                nodal[position] = nodal[position] + 0.5 * (
                    nodal[position - spacing] + nodal[(position + spacing) % GRID_A]
                )
            spacing //= 2
        for dom in range(dom_count):
            cut.put(out, comp * dom_count + dom, lambda p: nodal[dom * cut.planes + p])
        return carry

    lax.fori_loop(0, comp_count, send, 0)


def merge_columns(cut, columns, slabs, partners, weights, dom_count):
    comp_count = cut.count // dom_count
    tile = (cut.extent, HALF)
    return pl.pallas_call(
        functools.partial(merge_body, cut, dom_count),
        in_specs=[smem()] * 3 + [vmem()],
        out_specs=vmem(),
        out_shape=cut.shape(),
        scratch_shapes=[
            pltpu.VMEM((comp_count * GRID_A,) + tile, jnp.float32),
            pltpu.VMEM((comp_count * MULTI,) + tile, jnp.float32),
            pltpu.VMEM((SHARED,) + tile, jnp.float32),
            pltpu.VMEM((comp_count, GRID_A) + tile, jnp.float32),
        ],
        compiler_params=params(),
    )(slabs, partners, weights, columns)


def final_body(cut, weight, grid, changes, out, stage, sems):
    def copy(index):
        span = pl.ds(index * GROUP, GROUP)
        return pltpu.make_async_copy(stage.at[:, span], out.at[0, :, span], sems.at[index])

    def combine(index, carry):
        for row in range(GROUP):
            b = index * GROUP + row
            for chunk in range(cut.per_row):
                place = cut.place(chunk)
                for p, value in enumerate(cut.values(changes, b * cut.per_row + chunk)):
                    stage[(p, b) + place] = grid[(p, b) + place] * weight[0] + value
        copy(index).start()
        return carry

    lax.fori_loop(0, GRID_B // GROUP, combine, 0)
    for index in range(GRID_B // GROUP):
        copy(index).wait()


def final_planes(cut, grid, changes, weight):
    return pl.pallas_call(
        functools.partial(final_body, cut),
        in_specs=[smem(), vmem(), vmem()],
        out_specs=hbm(),
        out_shape=jax.ShapeDtypeStruct((1,) + grid.shape, jnp.float32),
        scratch_shapes=[
            pltpu.VMEM(grid.shape, jnp.float32),
            pltpu.SemaphoreType.DMA((GRID_B // GROUP,)),
        ],
        compiler_params=params(),
    )(weight, grid, changes)


def merge_tables(owner_lists, comp_count):
    held = owner_lists >= 0
    holders = jnp.sum(held.astype(jnp.int32), axis=1)
    is_shared = holders == comp_count
    is_pair = (holders > 1) & ~is_shared
    block = jnp.arange(owner_lists.shape[0], dtype=jnp.int32)
    earlier = (block[None, :] < block[:, None]) & is_shared[None, :]
    shared_rank = jnp.sum(earlier.astype(jnp.int32), axis=1)
    pair_total = jnp.sum(jnp.where(held, owner_lists, 0), axis=1)
    mark = jnp.where(is_shared, 1 + shared_rank, jnp.where(is_pair, 1 + SHARED + pair_total, 0))
    slab = jnp.arange(comp_count * GRID_A, dtype=jnp.int32)
    hits = owner_lists[None, :, :] == slab[:, None, None]
    marks = jnp.sum(jnp.where(hits, mark[None, :, None], 0), axis=(1, 2))
    paired = (marks > SHARED).reshape(comp_count, GRID_A)
    first = jnp.arange(GRID_A, dtype=jnp.int32)
    before = (first[None, :] < first[:, None])[None] & paired[:, None, :]
    pair_place = SHARED + jnp.sum(before.astype(jnp.int32), axis=2)
    place = jnp.where(paired, pair_place, marks.reshape(comp_count, GRID_A) - 1)
    partner = jnp.where(marks > SHARED, marks - 1 - SHARED - slab, -1)
    listed = (jnp.arange(comp_count, dtype=jnp.int32)[:, None] * MULTI + place).reshape(-1)
    partner_listed = jnp.sum(
        jnp.where(partner[:, None] == slab[None, :], listed[None, :], 0), axis=1
    ).reshape(comp_count, GRID_A)
    chosen = place[:, None, :] == jnp.arange(MULTI)[None, :, None]
    slabs = jnp.sum(jnp.where(chosen, first[None, None, :], 0), axis=2)
    partners = jnp.sum(jnp.where(chosen, partner_listed[:, None, :], 0), axis=2)
    return slabs, partners


def local(density, velocity, coefficients, owner_lists):
    comp_count, dom_count = lax.axis_size("comp"), lax.axis_size("dom")
    comp_index = lax.axis_index("comp")
    upward = [(i, (i + 1) % dom_count) for i in range(dom_count)]
    downward = [(target, source) for source, target in upward]

    slabs, partners = merge_tables(owner_lists, comp_count)
    weight = lax.dynamic_slice_in_dim(coefficients, comp_index, 1).astype(jnp.float32)
    matrix = lane_matrix()

    first, last = send_planes(density)
    for step in range(STEPS):
        low = lax.ppermute(last, "dom", upward)
        high = lax.ppermute(first, "dom", downward)
        if step == 0:
            partial, speeds = first_planes(density, matrix, velocity)
        else:
            partial = advance_planes(grid, matrix, speeds)
        if step < STEPS - 1:
            grid, first, last = edge_planes(partial, low, high, speeds)
    cut = Cut(comp_count * dom_count, density.shape[1])
    grid, columns = last_planes(cut, partial, low, high, speeds)
    columns = lax.all_to_all(columns, ("comp", "dom"), 0, 0, tiled=True)
    changes = merge_columns(cut, columns, slabs, partners, coefficients, dom_count)
    changes = lax.all_to_all(changes, ("comp", "dom"), 0, 0, tiled=True)
    return final_planes(cut, grid, changes, weight)


def solution(mesh):
    in_specs = (
        P("comp", "dom", None, None, None),
        P("comp", None, "dom", None, None, None),
        P(),
        P(),
    )
    out_specs = P("comp", "dom", None, None, None)
    return jax.shard_map(local, mesh=mesh, in_specs=in_specs, out_specs=out_specs, check_vma=False)
```

```python
import functools

import jax
import jax.numpy as jnp
import numpy as np
from jax import lax
from jax.experimental import pallas as pl
from jax.experimental.pallas import tpu as pltpu
from jax.sharding import PartitionSpec as P

GRID_A = 32
GRID_B = 16
GRID_C = 16
LANES = 256
HALF = 128
D_STRIDE = 32
LANE_AXES = ((8, 4), (4, 1))
STEPS = 4
GROUP = 4
SHARED = 4
BORROWED = 4
MULTI = 12
LEVELS = 32000.0
FINE = 16.0
TINY = 1e-36
VMEM_LIMIT = 24 * 1024 * 1024
MERGE_LIMIT = 60 * 1024 * 1024


def params(limit=VMEM_LIMIT):
    return pltpu.CompilerParams(vmem_limit_bytes=limit)


def smem():
    return pl.BlockSpec(memory_space=pltpu.SMEM)


def hbm():
    return pl.BlockSpec(memory_space=pltpu.HBM)


def vmem():
    return pl.BlockSpec(memory_space=pltpu.VMEM)


def code_of(peak):
    return jnp.ceil(jnp.log(jnp.maximum(peak, TINY)) * (FINE / 0.6931471805599453))


def encode(rows, put, put_code):
    peak = jnp.abs(rows[0]())
    for row in rows[1:]:
        peak = jnp.maximum(peak, jnp.abs(row()))
    code = code_of(peak)
    factor = jnp.exp2(code * (-1.0 / FINE)) * LEVELS
    put_code(code.astype(jnp.int32).astype(jnp.int16))
    for index, row in enumerate(rows):
        put(index, jnp.round(row() * factor).astype(jnp.int32).astype(jnp.int16))


def to_float(block):
    return block.astype(jnp.int32).astype(jnp.float32)


def unit_of(code_row):
    return jnp.exp2(to_float(code_row) * (1.0 / FINE)) * (1.0 / LEVELS)


def message_shape():
    return jax.ShapeDtypeStruct((GRID_B + 1, GRID_C, LANES), jnp.int16)


def code_plane(read, target):
    encode(
        [lambda b=b: read(b) for b in range(GRID_B)],
        lambda b, value: target.__setitem__(b, value),
        lambda value: target.__setitem__(GRID_B, value),
    )


def code_edges(odd, grid, inner, outer):
    planes = grid.shape[0]

    def work(to_next, to_last):
        code_plane(lambda b: grid[0, b], to_last)
        code_plane(lambda b: grid[planes - 1, b], to_next)

    @pl.when(odd[0] == 0)
    def _():
        work(inner, outer)

    @pl.when(odd[0] == 1)
    def _():
        work(outer, inner)


def send_planes(grid, odd):
    return pl.pallas_call(
        lambda odd, grid, inner, outer: code_edges(odd, grid, inner, outer),
        in_specs=[smem(), vmem()],
        out_specs=[vmem()] * 2,
        out_shape=[message_shape()] * 2,
        compiler_params=params(),
    )(odd, grid)


def lane_matrix():
    point = np.arange(LANES)
    eye = np.eye(LANES)
    total = np.zeros((LANES, LANES))
    differences = []
    for extent, stride in LANE_AXES:
        place = point // stride % extent
        forward = eye[:, point + ((place + 1) % extent - place) * stride]
        backward = eye[:, point + ((place - 1) % extent - place) * stride]
        total += forward + backward
        differences.append(forward - backward)
    matrix = np.concatenate([total] + differences, 1)
    return jnp.asarray(np.concatenate([matrix, matrix], 0), jnp.bfloat16)


def lane_products(plane, matrix, products):
    value = plane.reshape(GRID_B * GRID_C, LANES)
    coarse = value.astype(jnp.bfloat16)
    fine = (value - coarse.astype(jnp.float32)).astype(jnp.bfloat16)
    products[...] = jnp.dot(
        jnp.concatenate([coarse, fine], 1), matrix[...], preferred_element_type=jnp.float32
    )


def advance_body(grid, matrix, speeds, out, even, odd):
    planes = grid.shape[0]

    def rows(plane, products):
        up, down = jnp.minimum(plane + 1, planes - 1), jnp.maximum(plane - 1, 0)
        has_up = jnp.where(plane < planes - 1, 1.0, 0.0)
        has_down = jnp.where(plane > 0, 1.0, 0.0)
        for b in range(GRID_B):
            value = grid[plane, b]
            pairs = [
                (grid[up, b] * has_up, grid[down, b] * has_down),
                (grid[plane, (b + 1) % GRID_B], grid[plane, (b - 1) % GRID_B]),
                (pltpu.roll(value, GRID_C - 1, 0), pltpu.roll(value, 1, 0)),
                (pltpu.roll(value, LANES - D_STRIDE, 1), pltpu.roll(value, D_STRIDE, 1)),
            ]
            place = slice(b * GRID_C, (b + 1) * GRID_C)
            total = products[place, :LANES]
            drift = None
            for d in range(6):
                if d < len(pairs):
                    forward, backward = pairs[d]
                    total = total + (forward + backward)
                    difference = forward - backward
                else:
                    difference = products[place, (d - 3) * LANES : (d - 2) * LANES]
                term = speeds[d, plane, b].astype(jnp.float32) * difference
                drift = term if drift is None else drift + term
            out[plane, b] = 0.28 * value + 0.06 * total - 0.5 * drift

    lane_products(grid[0], matrix, even)

    def pair(index, carry):
        plane = 2 * index
        lane_products(grid[plane + 1], matrix, odd)
        rows(plane, even)
        lane_products(grid[jnp.minimum(plane + 2, planes - 1)], matrix, even)
        rows(plane + 1, odd)
        return carry

    lax.fori_loop(0, planes // 2, pair, 0)


def advance_planes(grid, matrix, velocity):
    points = grid.size
    products = pltpu.VMEM((GRID_B * GRID_C, matrix.shape[1]), jnp.float32)
    return pl.pallas_call(
        advance_body,
        in_specs=[vmem()] * 3,
        out_specs=vmem(),
        out_shape=jax.ShapeDtypeStruct(grid.shape, jnp.float32),
        scratch_shapes=[products, products],
        compiler_params=params(),
        cost_estimate=pl.CostEstimate(
            flops=1000 * points, bytes_accessed=20 * points, transcendentals=0
        ),
    )(grid, matrix, velocity)


def add_edges(odd, inner, outer, speeds, out):
    planes = out.shape[0]

    def work(from_next, from_last):
        for plane, source, sign in ((0, from_last, 0.5), (planes - 1, from_next, -0.5)):
            unit = unit_of(source[GRID_B])
            for b in range(GRID_B):
                share = 0.06 + sign * speeds[0, plane, b].astype(jnp.float32)
                out[plane, b] = out[plane, b] + to_float(source[b]) * unit * share

    @pl.when(odd[0] == 0)
    def _():
        work(inner, outer)

    @pl.when(odd[0] == 1)
    def _():
        work(outer, inner)


def edge_body(odd, partial, inner, outer, speeds, out, to_inner, to_outer):
    del partial
    add_edges(odd, inner, outer, speeds, out)
    code_edges(odd, out, to_inner, to_outer)


def edge_planes(odd, partial, inner, outer, speeds):
    return pl.pallas_call(
        edge_body,
        in_specs=[smem()] + [vmem()] * 4,
        out_specs=[vmem()] * 3,
        out_shape=[jax.ShapeDtypeStruct(partial.shape, jnp.float32)] + [message_shape()] * 2,
        input_output_aliases={1: 0},
        compiler_params=params(),
        cost_estimate=pl.CostEstimate(
            flops=2_000_000, bytes_accessed=2_000_000, transcendentals=0
        ),
    )(odd, partial, inner, outer, speeds)


class Cut:
    def __init__(self, count, planes):
        self.count, self.planes = count, planes
        self.splits = count // (2 * GRID_B)
        self.extent = GRID_C // self.splits
        self.code_rows = min(self.extent, 8)
        self.groups = self.extent // self.code_rows
        self.data_rows = planes * self.extent
        self.stack = min(planes, max(1, 16 // self.extent))
        self.per_row = 2 * self.splits

    def shape(self):
        return jax.ShapeDtypeStruct(
            (self.count, self.data_rows + self.code_rows, HALF), jnp.int16
        )

    def place(self, chunk):
        half, part = divmod(chunk, self.splits)
        return (
            slice(part * self.extent, (part + 1) * self.extent),
            slice(half * HALF, (half + 1) * HALF),
        )

    def spread(self, tile, repeats=1):
        return jnp.concatenate([tile] * (self.groups * repeats), 0)

    def put(self, target, chunk, value_of):
        peak = jnp.abs(value_of(0))
        for plane in range(1, self.planes):
            peak = jnp.maximum(peak, jnp.abs(value_of(plane)))
        top = peak[: self.code_rows]
        for group in range(1, self.groups):
            top = jnp.maximum(top, peak[group * self.code_rows : (group + 1) * self.code_rows])
        code = code_of(top)
        factor = self.spread(jnp.exp2(code * (-1.0 / FINE)) * LEVELS, self.stack)
        size = self.stack * self.extent
        for index in range(0, self.planes, self.stack):
            block = jnp.concatenate([value_of(index + i) for i in range(self.stack)], 0)
            start = index * self.extent
            target[chunk, start : start + size] = (
                jnp.round(block * factor).astype(jnp.int32).astype(jnp.int16)
            )
        target[chunk, self.data_rows :] = code.astype(jnp.int32).astype(jnp.int16)

    def values(self, source, chunk):
        unit = self.spread(unit_of(source[chunk, self.data_rows :]), self.stack)
        values = []
        size = self.stack * self.extent
        for index in range(0, self.planes, self.stack):
            start = index * self.extent
            block = to_float(source[chunk, start : start + size]) * unit
            for i in range(self.stack):
                values.append(block[i * self.extent : (i + 1) * self.extent])
        return values


def last_body(cut, odd, partial, inner, outer, speeds, grid, out):
    del partial
    add_edges(odd, inner, outer, speeds, grid)

    def pack(index, carry):
        for row in range(GROUP):
            b = index * GROUP + row
            for chunk in range(cut.per_row):
                place = cut.place(chunk)
                cut.put(out, b * cut.per_row + chunk, lambda p: grid[(p, b) + place])
        return carry

    lax.fori_loop(0, GRID_B // GROUP, pack, 0)


def last_planes(cut, odd, partial, inner, outer, speeds):
    return pl.pallas_call(
        functools.partial(last_body, cut),
        in_specs=[smem()] + [vmem()] * 4,
        out_specs=[vmem()] * 2,
        out_shape=[jax.ShapeDtypeStruct(partial.shape, jnp.float32), cut.shape()],
        input_output_aliases={1: 0},
        compiler_params=params(),
    )(odd, partial, inner, outer, speeds)


def merge_body(
    cut, dom_count, slabs, partners, weights, columns, out, values, rows, sums, grid, stage, sems
):
    comp_count = cut.count // dom_count

    def unpack(source, carry):
        for plane, value in enumerate(cut.values(columns, source)):
            values[source * cut.planes + plane] = value
        return carry

    lax.fori_loop(0, cut.count, unpack, 0, unroll=2)

    def gather(comp, carry):
        weight = weights[comp].astype(jnp.float32)
        base = comp * GRID_A
        for index in range(MULTI):
            slab = slabs[comp, index]
            spacing = slab & -slab
            share = jnp.where(slab > 0, -0.5 * weight, 0.0)
            near = (
                values[base + ((slab - spacing) & (GRID_A - 1))]
                + values[base + ((slab + spacing) & (GRID_A - 1))]
            )
            rows[comp * MULTI + index] = values[base + slab] * weight + near * share
        return carry

    lax.fori_loop(0, comp_count, gather, 0)
    for index in range(SHARED):
        total = rows[index]
        for comp in range(1, comp_count):
            total = total + rows[comp * MULTI + index]
        sums[index] = total
    grid[...] = jnp.zeros_like(grid)

    def scatter(comp, carry):
        for index in range(MULTI):
            if index < SHARED:
                change = sums[index] - rows[comp * MULTI + index]
            else:
                change = rows[partners[comp, index]]
            grid[comp, slabs[comp, index]] = change
        return carry

    lax.fori_loop(0, comp_count, scatter, 0)

    def copy(comp):
        span = pl.ds(comp * dom_count, dom_count)
        return pltpu.make_async_copy(stage.at[span], out.at[span], sems.at[comp])

    def send(comp, carry):
        nodal = [grid[comp, position] for position in range(GRID_A)]
        spacing = GRID_A // 2
        while spacing >= 1:
            for position in range(spacing, GRID_A, 2 * spacing):
                nodal[position] = nodal[position] + 0.5 * (
                    nodal[position - spacing] + nodal[(position + spacing) % GRID_A]
                )
            spacing //= 2
        for dom in range(dom_count):
            cut.put(stage, comp * dom_count + dom, lambda p: nodal[dom * cut.planes + p])
        copy(comp).start()
        return carry

    lax.fori_loop(0, comp_count, send, 0)
    for comp in range(comp_count):
        copy(comp).wait()


def merge_columns(cut, columns, slabs, partners, weights, dom_count):
    comp_count = cut.count // dom_count
    tile = (cut.extent, HALF)
    return pl.pallas_call(
        functools.partial(merge_body, cut, dom_count),
        in_specs=[smem()] * 3 + [vmem()],
        out_specs=hbm(),
        out_shape=cut.shape(),
        scratch_shapes=[
            pltpu.VMEM((comp_count * GRID_A,) + tile, jnp.float32),
            pltpu.VMEM((comp_count * MULTI,) + tile, jnp.float32),
            pltpu.VMEM((SHARED,) + tile, jnp.float32),
            pltpu.VMEM((comp_count, GRID_A) + tile, jnp.float32),
            pltpu.VMEM(cut.shape().shape, jnp.int16),
            pltpu.SemaphoreType.DMA((comp_count,)),
        ],
        compiler_params=params(MERGE_LIMIT),
    )(slabs, partners, weights, columns)


def final_body(cut, weight, grid, changes, out, stage, sems):
    def copy(index):
        span = pl.ds(index * GROUP, GROUP)
        return pltpu.make_async_copy(stage.at[:, span], out.at[0, :, span], sems.at[index])

    def combine(index, carry):
        for row in range(GROUP):
            b = index * GROUP + row
            for chunk in range(cut.per_row):
                place = cut.place(chunk)
                for p, value in enumerate(cut.values(changes, b * cut.per_row + chunk)):
                    stage[(p, b) + place] = grid[(p, b) + place] * weight[0] + value
        copy(index).start()
        return carry

    lax.fori_loop(0, GRID_B // GROUP, combine, 0)
    for index in range(GRID_B // GROUP):
        copy(index).wait()


def final_planes(cut, grid, changes, weight):
    return pl.pallas_call(
        functools.partial(final_body, cut),
        in_specs=[smem(), vmem(), vmem()],
        out_specs=hbm(),
        out_shape=jax.ShapeDtypeStruct((1,) + grid.shape, jnp.float32),
        scratch_shapes=[
            pltpu.VMEM(grid.shape, jnp.float32),
            pltpu.SemaphoreType.DMA((GRID_B // GROUP,)),
        ],
        compiler_params=params(),
    )(weight, grid, changes)


def merge_tables(owner_lists, comp_count):
    held = owner_lists >= 0
    holders = jnp.sum(held.astype(jnp.int32), axis=1)
    is_shared = holders == comp_count
    is_pair = (holders > 1) & ~is_shared
    block = jnp.arange(owner_lists.shape[0], dtype=jnp.int32)
    earlier = (block[None, :] < block[:, None]) & is_shared[None, :]
    shared_rank = jnp.sum(earlier.astype(jnp.int32), axis=1)
    pair_total = jnp.sum(jnp.where(held, owner_lists, 0), axis=1)
    mark = jnp.where(is_shared, 1 + shared_rank, jnp.where(is_pair, 1 + SHARED + pair_total, 0))
    slab = jnp.arange(comp_count * GRID_A, dtype=jnp.int32)
    hits = owner_lists[None, :, :] == slab[:, None, None]
    marks = jnp.sum(jnp.where(hits, mark[None, :, None], 0), axis=(1, 2))
    paired = (marks > SHARED).reshape(comp_count, GRID_A)
    first = jnp.arange(GRID_A, dtype=jnp.int32)
    before = (first[None, :] < first[:, None])[None] & paired[:, None, :]
    pair_place = SHARED + jnp.sum(before.astype(jnp.int32), axis=2)
    place = jnp.where(paired, pair_place, marks.reshape(comp_count, GRID_A) - 1)
    partner = jnp.where(marks > SHARED, marks - 1 - SHARED - slab, -1)
    listed = (jnp.arange(comp_count, dtype=jnp.int32)[:, None] * MULTI + place).reshape(-1)
    partner_listed = jnp.sum(
        jnp.where(partner[:, None] == slab[None, :], listed[None, :], 0), axis=1
    ).reshape(comp_count, GRID_A)
    chosen = place[:, None, :] == jnp.arange(MULTI)[None, :, None]
    slabs = jnp.sum(jnp.where(chosen, first[None, None, :], 0), axis=2)
    partners = jnp.sum(jnp.where(chosen, partner_listed[:, None, :], 0), axis=2)
    return slabs, partners


def local(density, velocity, coefficients, owner_lists):
    comp_count, dom_count = lax.axis_size("comp"), lax.axis_size("dom")
    comp_index = lax.axis_index("comp")
    inner_pairs = [(i, i ^ 1) for i in range(dom_count)]
    outer_pairs = [(i, (i - 1 + 2 * (i % 2)) % dom_count) for i in range(dom_count)]

    slabs, partners = merge_tables(owner_lists, comp_count)
    weight = lax.dynamic_slice_in_dim(coefficients, comp_index, 1).astype(jnp.float32)
    matrix = lane_matrix()

    odd = (lax.axis_index("dom") % 2).astype(jnp.int32).reshape(1)
    grid, speeds = density[0], velocity[0]
    to_inner, to_outer = send_planes(grid, odd)
    for step in range(STEPS):
        inner = lax.ppermute(to_inner, "dom", inner_pairs)
        outer = lax.ppermute(to_outer, "dom", outer_pairs)
        partial = advance_planes(grid, matrix, speeds)
        if step < STEPS - 1:
            grid, to_inner, to_outer = edge_planes(odd, partial, inner, outer, speeds)
    cut = Cut(comp_count * dom_count, density.shape[1])
    grid, columns = last_planes(cut, odd, partial, inner, outer, speeds)
    columns = lax.all_to_all(columns, ("comp", "dom"), 0, 0, tiled=True)
    changes = merge_columns(cut, columns, slabs, partners, coefficients, dom_count)
    changes = lax.all_to_all(changes, ("comp", "dom"), 0, 0, tiled=True)
    return final_planes(cut, grid, changes, weight)


def solution(mesh):
    in_specs = (
        P("comp", "dom", None, None, None),
        P("comp", None, "dom", None, None, None),
        P(),
        P(),
    )
    out_specs = P("comp", "dom", None, None, None)
    return jax.shard_map(local, mesh=mesh, in_specs=in_specs, out_specs=out_specs, check_vma=False)
```

```python
import functools

import jax
import jax.numpy as jnp
import numpy as np
from jax import lax
from jax.experimental import pallas as pl
from jax.experimental.pallas import tpu as pltpu
from jax.sharding import PartitionSpec as P

GRID_A = 32
GRID_B = 16
GRID_C = 16
LANES = 256
HALF = 128
D_STRIDE = 32
LANE_AXES = ((8, 4), (4, 1))
STEPS = 4
GROUP = 4
SHARED = 4
BORROWED = 4
MULTI = 12
LEVELS = 32000.0
FINE = 16.0
TINY = 1e-36
VMEM_LIMIT = 24 * 1024 * 1024


def params(limit=VMEM_LIMIT):
    return pltpu.CompilerParams(vmem_limit_bytes=limit)


def smem():
    return pl.BlockSpec(memory_space=pltpu.SMEM)


def hbm():
    return pl.BlockSpec(memory_space=pltpu.HBM)


def vmem():
    return pl.BlockSpec(memory_space=pltpu.VMEM)


def code_of(peak):
    return jnp.ceil(jnp.log(jnp.maximum(peak, TINY)) * (FINE / 0.6931471805599453))


def encode(rows, put, put_code):
    peak = jnp.abs(rows[0]())
    for row in rows[1:]:
        peak = jnp.maximum(peak, jnp.abs(row()))
    code = code_of(peak)
    factor = jnp.exp2(code * (-1.0 / FINE)) * LEVELS
    put_code(code.astype(jnp.int32).astype(jnp.int16))
    for index, row in enumerate(rows):
        put(index, jnp.round(row() * factor).astype(jnp.int32).astype(jnp.int16))


def to_float(block):
    return block.astype(jnp.int32).astype(jnp.float32)


def unit_of(code_row):
    return jnp.exp2(to_float(code_row) * (1.0 / FINE)) * (1.0 / LEVELS)


def message_shape():
    return jax.ShapeDtypeStruct((GRID_B + 1, GRID_C, LANES), jnp.int16)


def code_plane(read, target):
    encode(
        [lambda b=b: read(b) for b in range(GRID_B)],
        lambda b, value: target.__setitem__(b, value),
        lambda value: target.__setitem__(GRID_B, value),
    )


def code_edges(odd, grid, inner, outer):
    planes = grid.shape[0]

    def work(to_next, to_last):
        code_plane(lambda b: grid[0, b], to_last)
        code_plane(lambda b: grid[planes - 1, b], to_next)

    @pl.when(odd[0] == 0)
    def _():
        work(inner, outer)

    @pl.when(odd[0] == 1)
    def _():
        work(outer, inner)


def send_planes(grid, odd):
    return pl.pallas_call(
        lambda odd, grid, inner, outer: code_edges(odd, grid, inner, outer),
        in_specs=[smem(), vmem()],
        out_specs=[vmem()] * 2,
        out_shape=[message_shape()] * 2,
        compiler_params=params(),
    )(odd, grid)


def lane_matrix():
    point = np.arange(LANES)
    eye = np.eye(LANES)
    total = np.zeros((LANES, LANES))
    differences = []
    for extent, stride in LANE_AXES:
        place = point // stride % extent
        forward = eye[:, point + ((place + 1) % extent - place) * stride]
        backward = eye[:, point + ((place - 1) % extent - place) * stride]
        total += forward + backward
        differences.append(forward - backward)
    matrix = np.concatenate([total] + differences, 1)
    return jnp.asarray(np.concatenate([matrix, matrix], 0), jnp.bfloat16)


def lane_products(plane, matrix, products):
    value = plane.reshape(GRID_B * GRID_C, LANES)
    coarse = value.astype(jnp.bfloat16)
    fine = (value - coarse.astype(jnp.float32)).astype(jnp.bfloat16)
    products[...] = jnp.dot(
        jnp.concatenate([coarse, fine], 1), matrix[...], preferred_element_type=jnp.float32
    )


def advance_body(grid, matrix, speeds, out, even, odd):
    planes = grid.shape[0]

    def rows(plane, products):
        up, down = jnp.minimum(plane + 1, planes - 1), jnp.maximum(plane - 1, 0)
        has_up = jnp.where(plane < planes - 1, 1.0, 0.0)
        has_down = jnp.where(plane > 0, 1.0, 0.0)
        for b in range(GRID_B):
            value = grid[plane, b]
            pairs = [
                (grid[up, b] * has_up, grid[down, b] * has_down),
                (grid[plane, (b + 1) % GRID_B], grid[plane, (b - 1) % GRID_B]),
                (pltpu.roll(value, GRID_C - 1, 0), pltpu.roll(value, 1, 0)),
                (pltpu.roll(value, LANES - D_STRIDE, 1), pltpu.roll(value, D_STRIDE, 1)),
            ]
            place = slice(b * GRID_C, (b + 1) * GRID_C)
            total = products[place, :LANES]
            drift = None
            for d in range(6):
                if d < len(pairs):
                    forward, backward = pairs[d]
                    total = total + (forward + backward)
                    difference = forward - backward
                else:
                    difference = products[place, (d - 3) * LANES : (d - 2) * LANES]
                term = speeds[d, plane, b].astype(jnp.float32) * difference
                drift = term if drift is None else drift + term
            out[plane, b] = 0.28 * value + 0.06 * total - 0.5 * drift

    lane_products(grid[0], matrix, even)

    def pair(index, carry):
        plane = 2 * index
        lane_products(grid[plane + 1], matrix, odd)
        rows(plane, even)
        lane_products(grid[jnp.minimum(plane + 2, planes - 1)], matrix, even)
        rows(plane + 1, odd)
        return carry

    lax.fori_loop(0, planes // 2, pair, 0)


def advance_planes(grid, matrix, velocity):
    points = grid.size
    products = pltpu.VMEM((GRID_B * GRID_C, matrix.shape[1]), jnp.float32)
    return pl.pallas_call(
        advance_body,
        in_specs=[vmem()] * 3,
        out_specs=vmem(),
        out_shape=jax.ShapeDtypeStruct(grid.shape, jnp.float32),
        scratch_shapes=[products, products],
        compiler_params=params(),
        cost_estimate=pl.CostEstimate(
            flops=1000 * points, bytes_accessed=20 * points, transcendentals=0
        ),
    )(grid, matrix, velocity)


def add_edges(odd, inner, outer, speeds, out):
    planes = out.shape[0]

    def work(from_next, from_last):
        for plane, source, sign in ((0, from_last, 0.5), (planes - 1, from_next, -0.5)):
            unit = unit_of(source[GRID_B])
            for b in range(GRID_B):
                share = 0.06 + sign * speeds[0, plane, b].astype(jnp.float32)
                out[plane, b] = out[plane, b] + to_float(source[b]) * unit * share

    @pl.when(odd[0] == 0)
    def _():
        work(inner, outer)

    @pl.when(odd[0] == 1)
    def _():
        work(outer, inner)


def edge_body(odd, partial, inner, outer, speeds, out, to_inner, to_outer):
    del partial
    add_edges(odd, inner, outer, speeds, out)
    code_edges(odd, out, to_inner, to_outer)


def edge_planes(odd, partial, inner, outer, speeds):
    return pl.pallas_call(
        edge_body,
        in_specs=[smem()] + [vmem()] * 4,
        out_specs=[vmem()] * 3,
        out_shape=[jax.ShapeDtypeStruct(partial.shape, jnp.float32)] + [message_shape()] * 2,
        input_output_aliases={1: 0},
        compiler_params=params(),
        cost_estimate=pl.CostEstimate(
            flops=2_000_000, bytes_accessed=2_000_000, transcendentals=0
        ),
    )(odd, partial, inner, outer, speeds)


class Cut:
    def __init__(self, count, planes):
        self.count, self.planes = count, planes
        self.splits = count // (2 * GRID_B)
        self.extent = GRID_C // self.splits
        self.code_rows = min(self.extent, 8)
        self.groups = self.extent // self.code_rows
        self.data_rows = planes * self.extent
        self.stack = min(planes, max(1, 16 // self.extent))
        self.per_row = 2 * self.splits

    def shape(self):
        return jax.ShapeDtypeStruct(
            (self.count, self.data_rows + self.code_rows, HALF), jnp.int16
        )

    def place(self, chunk):
        half, part = divmod(chunk, self.splits)
        return (
            slice(part * self.extent, (part + 1) * self.extent),
            slice(half * HALF, (half + 1) * HALF),
        )

    def spread(self, tile, repeats=1):
        return jnp.concatenate([tile] * (self.groups * repeats), 0)

    def put(self, target, chunk, value_of):
        peak = jnp.abs(value_of(0))
        for plane in range(1, self.planes):
            peak = jnp.maximum(peak, jnp.abs(value_of(plane)))
        top = peak[: self.code_rows]
        for group in range(1, self.groups):
            top = jnp.maximum(top, peak[group * self.code_rows : (group + 1) * self.code_rows])
        code = code_of(top)
        factor = self.spread(jnp.exp2(code * (-1.0 / FINE)) * LEVELS, self.stack)
        size = self.stack * self.extent
        for index in range(0, self.planes, self.stack):
            block = jnp.concatenate([value_of(index + i) for i in range(self.stack)], 0)
            start = index * self.extent
            target[chunk, start : start + size] = (
                jnp.round(block * factor).astype(jnp.int32).astype(jnp.int16)
            )
        target[chunk, self.data_rows :] = code.astype(jnp.int32).astype(jnp.int16)

    def values(self, source, chunk):
        unit = self.spread(unit_of(source[chunk, self.data_rows :]), self.stack)
        values = []
        size = self.stack * self.extent
        for index in range(0, self.planes, self.stack):
            start = index * self.extent
            block = to_float(source[chunk, start : start + size]) * unit
            for i in range(self.stack):
                values.append(block[i * self.extent : (i + 1) * self.extent])
        return values


def last_body(cut, odd, partial, inner, outer, speeds, grid, out):
    del partial
    add_edges(odd, inner, outer, speeds, grid)

    def pack(index, carry):
        for row in range(GROUP):
            b = index * GROUP + row
            for chunk in range(cut.per_row):
                place = cut.place(chunk)
                cut.put(out, b * cut.per_row + chunk, lambda p: grid[(p, b) + place])
        return carry

    lax.fori_loop(0, GRID_B // GROUP, pack, 0)


def last_planes(cut, odd, partial, inner, outer, speeds):
    return pl.pallas_call(
        functools.partial(last_body, cut),
        in_specs=[smem()] + [vmem()] * 4,
        out_specs=[vmem()] * 2,
        out_shape=[jax.ShapeDtypeStruct(partial.shape, jnp.float32), cut.shape()],
        input_output_aliases={1: 0},
        compiler_params=params(),
    )(odd, partial, inner, outer, speeds)


def merge_body(
    cut, dom_count, slabs, partners, weights, columns, out, values, rows, sums, grid
):
    comp_count = cut.count // dom_count

    def unpack(source, carry):
        for plane, value in enumerate(cut.values(columns, source)):
            values[source * cut.planes + plane] = value
        return carry

    lax.fori_loop(0, cut.count, unpack, 0, unroll=2)

    def gather(comp, carry):
        weight = weights[comp].astype(jnp.float32)
        base = comp * GRID_A
        for index in range(MULTI):
            slab = slabs[comp, index]
            spacing = slab & -slab
            share = jnp.where(slab > 0, -0.5 * weight, 0.0)
            near = (
                values[base + ((slab - spacing) & (GRID_A - 1))]
                + values[base + ((slab + spacing) & (GRID_A - 1))]
            )
            rows[comp * MULTI + index] = values[base + slab] * weight + near * share
        return carry

    lax.fori_loop(0, comp_count, gather, 0)
    for index in range(SHARED):
        total = rows[index]
        for comp in range(1, comp_count):
            total = total + rows[comp * MULTI + index]
        sums[index] = total
    grid[...] = jnp.zeros_like(grid)

    def scatter(comp, carry):
        for index in range(MULTI):
            if index < SHARED:
                change = sums[index] - rows[comp * MULTI + index]
            else:
                change = rows[partners[comp, index]]
            grid[comp, slabs[comp, index]] = change
        return carry

    lax.fori_loop(0, comp_count, scatter, 0)

    def send(comp, carry):
        nodal = [grid[comp, position] for position in range(GRID_A)]
        spacing = GRID_A // 2
        while spacing >= 1:
            for position in range(spacing, GRID_A, 2 * spacing):
                nodal[position] = nodal[position] + 0.5 * (
                    nodal[position - spacing] + nodal[(position + spacing) % GRID_A]
                )
            spacing //= 2
        for dom in range(dom_count):
            cut.put(out, comp * dom_count + dom, lambda p: nodal[dom * cut.planes + p])
        return carry

    lax.fori_loop(0, comp_count, send, 0)


def merge_columns(cut, columns, slabs, partners, weights, dom_count):
    comp_count = cut.count // dom_count
    tile = (cut.extent, HALF)
    return pl.pallas_call(
        functools.partial(merge_body, cut, dom_count),
        in_specs=[smem()] * 3 + [vmem()],
        out_specs=vmem(),
        out_shape=cut.shape(),
        scratch_shapes=[
            pltpu.VMEM((comp_count * GRID_A,) + tile, jnp.float32),
            pltpu.VMEM((comp_count * MULTI,) + tile, jnp.float32),
            pltpu.VMEM((SHARED,) + tile, jnp.float32),
            pltpu.VMEM((comp_count, GRID_A) + tile, jnp.float32),
        ],
        compiler_params=params(),
    )(slabs, partners, weights, columns)


def final_body(cut, weight, grid, changes, out, stage, sems):
    def copy(index):
        span = pl.ds(index * GROUP, GROUP)
        return pltpu.make_async_copy(stage.at[:, span], out.at[0, :, span], sems.at[index])

    def combine(index, carry):
        for row in range(GROUP):
            b = index * GROUP + row
            for chunk in range(cut.per_row):
                place = cut.place(chunk)
                for p, value in enumerate(cut.values(changes, b * cut.per_row + chunk)):
                    stage[(p, b) + place] = grid[(p, b) + place] * weight[0] + value
        copy(index).start()
        return carry

    lax.fori_loop(0, GRID_B // GROUP, combine, 0)
    for index in range(GRID_B // GROUP):
        copy(index).wait()


def final_planes(cut, grid, changes, weight):
    return pl.pallas_call(
        functools.partial(final_body, cut),
        in_specs=[smem(), vmem(), vmem()],
        out_specs=hbm(),
        out_shape=jax.ShapeDtypeStruct((1,) + grid.shape, jnp.float32),
        scratch_shapes=[
            pltpu.VMEM(grid.shape, jnp.float32),
            pltpu.SemaphoreType.DMA((GRID_B // GROUP,)),
        ],
        compiler_params=params(),
    )(weight, grid, changes)


def merge_tables(owner_lists, comp_count):
    held = owner_lists >= 0
    holders = jnp.sum(held.astype(jnp.int32), axis=1)
    is_shared = holders == comp_count
    is_pair = (holders > 1) & ~is_shared
    block = jnp.arange(owner_lists.shape[0], dtype=jnp.int32)
    earlier = (block[None, :] < block[:, None]) & is_shared[None, :]
    shared_rank = jnp.sum(earlier.astype(jnp.int32), axis=1)
    pair_total = jnp.sum(jnp.where(held, owner_lists, 0), axis=1)
    mark = jnp.where(is_shared, 1 + shared_rank, jnp.where(is_pair, 1 + SHARED + pair_total, 0))
    slab = jnp.arange(comp_count * GRID_A, dtype=jnp.int32)
    hits = owner_lists[None, :, :] == slab[:, None, None]
    marks = jnp.sum(jnp.where(hits, mark[None, :, None], 0), axis=(1, 2))
    paired = (marks > SHARED).reshape(comp_count, GRID_A)
    first = jnp.arange(GRID_A, dtype=jnp.int32)
    before = (first[None, :] < first[:, None])[None] & paired[:, None, :]
    pair_place = SHARED + jnp.sum(before.astype(jnp.int32), axis=2)
    place = jnp.where(paired, pair_place, marks.reshape(comp_count, GRID_A) - 1)
    partner = jnp.where(marks > SHARED, marks - 1 - SHARED - slab, -1)
    listed = (jnp.arange(comp_count, dtype=jnp.int32)[:, None] * MULTI + place).reshape(-1)
    partner_listed = jnp.sum(
        jnp.where(partner[:, None] == slab[None, :], listed[None, :], 0), axis=1
    ).reshape(comp_count, GRID_A)
    chosen = place[:, None, :] == jnp.arange(MULTI)[None, :, None]
    slabs = jnp.sum(jnp.where(chosen, first[None, None, :], 0), axis=2)
    partners = jnp.sum(jnp.where(chosen, partner_listed[:, None, :], 0), axis=2)
    return slabs, partners


def local(density, velocity, coefficients, owner_lists):
    comp_count, dom_count = lax.axis_size("comp"), lax.axis_size("dom")
    comp_index = lax.axis_index("comp")
    inner_pairs = [(i, i ^ 1) for i in range(dom_count)]
    outer_pairs = [(i, (i - 1 + 2 * (i % 2)) % dom_count) for i in range(dom_count)]

    slabs, partners = merge_tables(owner_lists, comp_count)
    weight = lax.dynamic_slice_in_dim(coefficients, comp_index, 1).astype(jnp.float32)
    matrix = lane_matrix()

    odd = (lax.axis_index("dom") % 2).astype(jnp.int32).reshape(1)
    grid, speeds = density[0], velocity[0]
    to_inner, to_outer = send_planes(grid, odd)
    for step in range(STEPS):
        inner = lax.ppermute(to_inner, "dom", inner_pairs)
        outer = lax.ppermute(to_outer, "dom", outer_pairs)
        partial = advance_planes(grid, matrix, speeds)
        if step < STEPS - 1:
            grid, to_inner, to_outer = edge_planes(odd, partial, inner, outer, speeds)
    cut = Cut(comp_count * dom_count, density.shape[1])
    grid, columns = last_planes(cut, odd, partial, inner, outer, speeds)
    columns = lax.all_to_all(columns, ("comp", "dom"), 0, 0, tiled=True)
    changes = merge_columns(cut, columns, slabs, partners, coefficients, dom_count)
    changes = lax.all_to_all(changes, ("comp", "dom"), 0, 0, tiled=True)
    return final_planes(cut, grid, changes, weight)


def solution(mesh):
    in_specs = (
        P("comp", "dom", None, None, None),
        P("comp", None, "dom", None, None, None),
        P(),
        P(),
    )
    out_specs = P("comp", "dom", None, None, None)
    return jax.shard_map(local, mesh=mesh, in_specs=in_specs, out_specs=out_specs, check_vma=False)
```

```python
import functools

import jax
import jax.numpy as jnp
import numpy as np
from jax import lax
from jax.experimental import pallas as pl
from jax.experimental.pallas import tpu as pltpu
from jax.sharding import PartitionSpec as P

GRID_A = 32
GRID_B = 16
GRID_C = 16
LANES = 256
HALF = 128
D_STRIDE = 32
LANE_AXES = ((8, 4), (4, 1))
STEPS = 4
GROUP = 4
SHARED = 4
BORROWED = 4
MULTI = 12
LEVELS = 32000.0
FINE = 16.0
TINY = 1e-36
VMEM_LIMIT = 24 * 1024 * 1024
FIRST_LIMIT = 40 * 1024 * 1024


def params(limit=VMEM_LIMIT):
    return pltpu.CompilerParams(vmem_limit_bytes=limit)


def smem():
    return pl.BlockSpec(memory_space=pltpu.SMEM)


def hbm():
    return pl.BlockSpec(memory_space=pltpu.HBM)


def vmem():
    return pl.BlockSpec(memory_space=pltpu.VMEM)


def code_of(peak):
    return jnp.ceil(jnp.log(jnp.maximum(peak, TINY)) * (FINE / 0.6931471805599453))


def encode(rows, put, put_code):
    peak = jnp.abs(rows[0]())
    for row in rows[1:]:
        peak = jnp.maximum(peak, jnp.abs(row()))
    code = code_of(peak)
    factor = jnp.exp2(code * (-1.0 / FINE)) * LEVELS
    put_code(code.astype(jnp.int32).astype(jnp.int16))
    for index, row in enumerate(rows):
        put(index, jnp.round(row() * factor).astype(jnp.int32).astype(jnp.int16))


def to_float(block):
    return block.astype(jnp.int32).astype(jnp.float32)


def unit_of(code_row):
    return jnp.exp2(to_float(code_row) * (1.0 / FINE)) * (1.0 / LEVELS)


def message_shape():
    return jax.ShapeDtypeStruct((GRID_B + 1, GRID_C, LANES), jnp.int16)


def code_plane(read, target):
    encode(
        [lambda b=b: read(b) for b in range(GRID_B)],
        lambda b, value: target.__setitem__(b, value),
        lambda value: target.__setitem__(GRID_B, value),
    )


def code_edges(odd, grid, inner, outer):
    planes = grid.shape[0]

    def work(to_next, to_last):
        code_plane(lambda b: grid[0, b], to_last)
        code_plane(lambda b: grid[planes - 1, b], to_next)

    @pl.when(odd[0] == 0)
    def _():
        work(inner, outer)

    @pl.when(odd[0] == 1)
    def _():
        work(outer, inner)


def send_planes(grid, odd):
    return pl.pallas_call(
        lambda odd, grid, inner, outer: code_edges(odd, grid, inner, outer),
        in_specs=[smem(), vmem()],
        out_specs=[vmem()] * 2,
        out_shape=[message_shape()] * 2,
        compiler_params=params(),
    )(odd, grid)


def lane_matrix():
    point = np.arange(LANES)
    eye = np.eye(LANES)
    total = np.zeros((LANES, LANES))
    differences = []
    for extent, stride in LANE_AXES:
        place = point // stride % extent
        forward = eye[:, point + ((place + 1) % extent - place) * stride]
        backward = eye[:, point + ((place - 1) % extent - place) * stride]
        total += forward + backward
        differences.append(forward - backward)
    matrix = np.concatenate([total] + differences, 1)
    return jnp.asarray(np.concatenate([matrix, matrix], 0), jnp.bfloat16)


def lane_products(plane, matrix, products):
    value = plane.reshape(GRID_B * GRID_C, LANES)
    coarse = value.astype(jnp.bfloat16)
    fine = (value - coarse.astype(jnp.float32)).astype(jnp.bfloat16)
    products[...] = jnp.dot(
        jnp.concatenate([coarse, fine], 1), matrix[...], preferred_element_type=jnp.float32
    )


def advance(grid, matrix, speeds, out, even, odd, ready):
    planes = grid.shape[0]

    def rows(plane, products):
        up, down = jnp.minimum(plane + 1, planes - 1), jnp.maximum(plane - 1, 0)
        has_up = jnp.where(plane < planes - 1, 1.0, 0.0)
        has_down = jnp.where(plane > 0, 1.0, 0.0)
        for b in range(GRID_B):
            value = grid[plane, b]
            pairs = [
                (grid[up, b] * has_up, grid[down, b] * has_down),
                (grid[plane, (b + 1) % GRID_B], grid[plane, (b - 1) % GRID_B]),
                (pltpu.roll(value, GRID_C - 1, 0), pltpu.roll(value, 1, 0)),
                (pltpu.roll(value, LANES - D_STRIDE, 1), pltpu.roll(value, D_STRIDE, 1)),
            ]
            place = slice(b * GRID_C, (b + 1) * GRID_C)
            total = products[place, :LANES]
            drift = None
            for d in range(6):
                if d < len(pairs):
                    forward, backward = pairs[d]
                    total = total + (forward + backward)
                    difference = forward - backward
                else:
                    difference = products[place, (d - 3) * LANES : (d - 2) * LANES]
                term = speeds[d, plane, b].astype(jnp.float32) * difference
                drift = term if drift is None else drift + term
            out[plane, b] = 0.28 * value + 0.06 * total - 0.5 * drift

    lane_products(grid[0], matrix, even)

    def pair(index, carry):
        plane = 2 * index
        ready(plane)
        lane_products(grid[plane + 1], matrix, odd)
        rows(plane, even)
        ready(plane + 1)
        lane_products(grid[jnp.minimum(plane + 2, planes - 1)], matrix, even)
        rows(plane + 1, odd)
        return carry

    lax.fori_loop(0, planes // 2, pair, 0)


def advance_body(grid, matrix, speeds, out, even, odd):
    advance(grid, matrix, speeds, out, even, odd, lambda plane: None)


def first_body(grid, matrix, velocity, out, speeds, even, odd, sems):
    planes = grid.shape[0]

    def copy(plane):
        return pltpu.make_async_copy(velocity.at[0, :, plane], speeds.at[:, plane], sems.at[plane])

    for plane in range(planes):
        copy(plane).start()
    advance(grid, matrix, speeds, out, even, odd, lambda plane: copy(plane).wait())


def first_planes(grid, matrix, velocity):
    products = pltpu.VMEM((GRID_B * GRID_C, matrix.shape[1]), jnp.float32)
    return pl.pallas_call(
        first_body,
        in_specs=[vmem(), vmem(), hbm()],
        out_specs=[vmem()] * 2,
        out_shape=[
            jax.ShapeDtypeStruct(grid.shape, jnp.float32),
            jax.ShapeDtypeStruct(velocity.shape[1:], jnp.bfloat16),
        ],
        scratch_shapes=[products, products, pltpu.SemaphoreType.DMA((grid.shape[0],))],
        compiler_params=params(FIRST_LIMIT),
        cost_estimate=pl.CostEstimate(
            flops=1000 * grid.size, bytes_accessed=20 * grid.size, transcendentals=0
        ),
    )(grid, matrix, velocity)


def advance_planes(grid, matrix, velocity):
    points = grid.size
    products = pltpu.VMEM((GRID_B * GRID_C, matrix.shape[1]), jnp.float32)
    return pl.pallas_call(
        advance_body,
        in_specs=[vmem()] * 3,
        out_specs=vmem(),
        out_shape=jax.ShapeDtypeStruct(grid.shape, jnp.float32),
        scratch_shapes=[products, products],
        compiler_params=params(),
        cost_estimate=pl.CostEstimate(
            flops=1000 * points, bytes_accessed=20 * points, transcendentals=0
        ),
    )(grid, matrix, velocity)


def add_edges(odd, inner, outer, speeds, out):
    planes = out.shape[0]

    def work(from_next, from_last):
        for plane, source, sign in ((0, from_last, 0.5), (planes - 1, from_next, -0.5)):
            unit = unit_of(source[GRID_B])
            for b in range(GRID_B):
                share = 0.06 + sign * speeds[0, plane, b].astype(jnp.float32)
                out[plane, b] = out[plane, b] + to_float(source[b]) * unit * share

    @pl.when(odd[0] == 0)
    def _():
        work(inner, outer)

    @pl.when(odd[0] == 1)
    def _():
        work(outer, inner)


def edge_body(odd, partial, inner, outer, speeds, out, to_inner, to_outer):
    del partial
    add_edges(odd, inner, outer, speeds, out)
    code_edges(odd, out, to_inner, to_outer)


def edge_planes(odd, partial, inner, outer, speeds):
    return pl.pallas_call(
        edge_body,
        in_specs=[smem()] + [vmem()] * 4,
        out_specs=[vmem()] * 3,
        out_shape=[jax.ShapeDtypeStruct(partial.shape, jnp.float32)] + [message_shape()] * 2,
        input_output_aliases={1: 0},
        compiler_params=params(),
        cost_estimate=pl.CostEstimate(
            flops=2_000_000, bytes_accessed=2_000_000, transcendentals=0
        ),
    )(odd, partial, inner, outer, speeds)


class Cut:
    def __init__(self, count, planes):
        self.count, self.planes = count, planes
        self.splits = count // (2 * GRID_B)
        self.extent = GRID_C // self.splits
        self.code_rows = min(self.extent, 8)
        self.groups = self.extent // self.code_rows
        self.data_rows = planes * self.extent
        self.stack = min(planes, max(1, 16 // self.extent))
        self.per_row = 2 * self.splits

    def shape(self):
        return jax.ShapeDtypeStruct(
            (self.count, self.data_rows + self.code_rows, HALF), jnp.int16
        )

    def place(self, chunk):
        half, part = divmod(chunk, self.splits)
        return (
            slice(part * self.extent, (part + 1) * self.extent),
            slice(half * HALF, (half + 1) * HALF),
        )

    def spread(self, tile, repeats=1):
        return jnp.concatenate([tile] * (self.groups * repeats), 0)

    def put(self, target, chunk, value_of):
        peak = jnp.abs(value_of(0))
        for plane in range(1, self.planes):
            peak = jnp.maximum(peak, jnp.abs(value_of(plane)))
        top = peak[: self.code_rows]
        for group in range(1, self.groups):
            top = jnp.maximum(top, peak[group * self.code_rows : (group + 1) * self.code_rows])
        code = code_of(top)
        factor = self.spread(jnp.exp2(code * (-1.0 / FINE)) * LEVELS, self.stack)
        size = self.stack * self.extent
        for index in range(0, self.planes, self.stack):
            block = jnp.concatenate([value_of(index + i) for i in range(self.stack)], 0)
            start = index * self.extent
            target[chunk, start : start + size] = (
                jnp.round(block * factor).astype(jnp.int32).astype(jnp.int16)
            )
        target[chunk, self.data_rows :] = code.astype(jnp.int32).astype(jnp.int16)

    def values(self, source, chunk):
        unit = self.spread(unit_of(source[chunk, self.data_rows :]), self.stack)
        values = []
        size = self.stack * self.extent
        for index in range(0, self.planes, self.stack):
            start = index * self.extent
            block = to_float(source[chunk, start : start + size]) * unit
            for i in range(self.stack):
                values.append(block[i * self.extent : (i + 1) * self.extent])
        return values


def last_body(cut, odd, partial, inner, outer, speeds, grid, out):
    del partial
    add_edges(odd, inner, outer, speeds, grid)

    def pack(index, carry):
        for row in range(GROUP):
            b = index * GROUP + row
            for chunk in range(cut.per_row):
                place = cut.place(chunk)
                cut.put(out, b * cut.per_row + chunk, lambda p: grid[(p, b) + place])
        return carry

    lax.fori_loop(0, GRID_B // GROUP, pack, 0)


def last_planes(cut, odd, partial, inner, outer, speeds):
    return pl.pallas_call(
        functools.partial(last_body, cut),
        in_specs=[smem()] + [vmem()] * 4,
        out_specs=[vmem()] * 2,
        out_shape=[jax.ShapeDtypeStruct(partial.shape, jnp.float32), cut.shape()],
        input_output_aliases={1: 0},
        compiler_params=params(),
    )(odd, partial, inner, outer, speeds)


def merge_body(
    cut, dom_count, slabs, partners, weights, columns, out, values, rows, sums, grid
):
    comp_count = cut.count // dom_count

    def unpack(source, carry):
        for plane, value in enumerate(cut.values(columns, source)):
            values[source * cut.planes + plane] = value
        return carry

    lax.fori_loop(0, cut.count, unpack, 0, unroll=2)

    def gather(comp, carry):
        weight = weights[comp].astype(jnp.float32)
        base = comp * GRID_A
        for index in range(MULTI):
            slab = slabs[comp, index]
            spacing = slab & -slab
            share = jnp.where(slab > 0, -0.5 * weight, 0.0)
            near = (
                values[base + ((slab - spacing) & (GRID_A - 1))]
                + values[base + ((slab + spacing) & (GRID_A - 1))]
            )
            rows[comp * MULTI + index] = values[base + slab] * weight + near * share
        return carry

    lax.fori_loop(0, comp_count, gather, 0)
    for index in range(SHARED):
        total = rows[index]
        for comp in range(1, comp_count):
            total = total + rows[comp * MULTI + index]
        sums[index] = total
    grid[...] = jnp.zeros_like(grid)

    def scatter(comp, carry):
        for index in range(MULTI):
            if index < SHARED:
                change = sums[index] - rows[comp * MULTI + index]
            else:
                change = rows[partners[comp, index]]
            grid[comp, slabs[comp, index]] = change
        return carry

    lax.fori_loop(0, comp_count, scatter, 0)

    def send(comp, carry):
        nodal = [grid[comp, position] for position in range(GRID_A)]
        spacing = GRID_A // 2
        while spacing >= 1:
            for position in range(spacing, GRID_A, 2 * spacing):
                nodal[position] = nodal[position] + 0.5 * (
                    nodal[position - spacing] + nodal[(position + spacing) % GRID_A]
                )
            spacing //= 2
        for dom in range(dom_count):
            cut.put(out, comp * dom_count + dom, lambda p: nodal[dom * cut.planes + p])
        return carry

    lax.fori_loop(0, comp_count, send, 0)


def merge_columns(cut, columns, slabs, partners, weights, dom_count):
    comp_count = cut.count // dom_count
    tile = (cut.extent, HALF)
    return pl.pallas_call(
        functools.partial(merge_body, cut, dom_count),
        in_specs=[smem()] * 3 + [vmem()],
        out_specs=vmem(),
        out_shape=cut.shape(),
        scratch_shapes=[
            pltpu.VMEM((comp_count * GRID_A,) + tile, jnp.float32),
            pltpu.VMEM((comp_count * MULTI,) + tile, jnp.float32),
            pltpu.VMEM((SHARED,) + tile, jnp.float32),
            pltpu.VMEM((comp_count, GRID_A) + tile, jnp.float32),
        ],
        compiler_params=params(),
    )(slabs, partners, weights, columns)


def final_body(cut, weights, comp, grid, changes, out, stage, sems):
    weight = weights[comp[0]].astype(jnp.float32)

    def copy(index):
        span = pl.ds(index * GROUP, GROUP)
        return pltpu.make_async_copy(stage.at[:, span], out.at[0, :, span], sems.at[index])

    def combine(index, carry):
        for row in range(GROUP):
            b = index * GROUP + row
            for chunk in range(cut.per_row):
                place = cut.place(chunk)
                for p, value in enumerate(cut.values(changes, b * cut.per_row + chunk)):
                    stage[(p, b) + place] = grid[(p, b) + place] * weight + value
        copy(index).start()
        return carry

    lax.fori_loop(0, GRID_B // GROUP, combine, 0)
    for index in range(GRID_B // GROUP):
        copy(index).wait()


def final_planes(cut, grid, changes, weights, comp):
    return pl.pallas_call(
        functools.partial(final_body, cut),
        in_specs=[smem(), smem(), vmem(), vmem()],
        out_specs=hbm(),
        out_shape=jax.ShapeDtypeStruct((1,) + grid.shape, jnp.float32),
        scratch_shapes=[
            pltpu.VMEM(grid.shape, jnp.float32),
            pltpu.SemaphoreType.DMA((GRID_B // GROUP,)),
        ],
        compiler_params=params(),
    )(weights, comp, grid, changes)


def tables_body(owners, slabs, partners, places):
    blocks = owners.shape[0]
    comp_count = slabs.shape[0]

    def clear(comp, carry):
        places[comp] = SHARED
        for index in range(SHARED):
            partners[comp, index] = 0
        return carry

    lax.fori_loop(0, comp_count, clear, 0)

    def block(number, shared):
        first, second = owners[number, 0], owners[number, 1]
        is_shared = owners[number, 2] >= 0

        @pl.when((second >= 0) & ~is_shared)
        def _():
            comps = [lax.div(slab, GRID_A) for slab in (first, second)]
            own = [places[comp] for comp in comps]
            for side, slab in enumerate((first, second)):
                slabs[comps[side], own[side]] = lax.rem(slab, GRID_A)
                partners[comps[side], own[side]] = comps[1 - side] * MULTI + own[1 - side]
                places[comps[side]] = own[side] + 1

        @pl.when(is_shared)
        def _():
            def holder(index, carry):
                slab = owners[number, index]
                slabs[lax.div(slab, GRID_A), shared] = lax.rem(slab, GRID_A)
                return carry

            lax.fori_loop(0, comp_count, holder, 0)

        return shared + jnp.where(is_shared, 1, 0)

    lax.fori_loop(0, blocks, block, 0)


def merge_tables(owner_lists, comp_count):
    shape = jax.ShapeDtypeStruct((comp_count, MULTI), jnp.int32)
    return pl.pallas_call(
        tables_body,
        in_specs=[smem()],
        out_specs=[smem()] * 2,
        out_shape=[shape] * 2,
        scratch_shapes=[pltpu.SMEM((comp_count,), jnp.int32)],
    )(owner_lists)


def local(density, velocity, coefficients, owner_lists):
    comp_count, dom_count = lax.axis_size("comp"), lax.axis_size("dom")
    inner_pairs = [(i, i ^ 1) for i in range(dom_count)]
    outer_pairs = [(i, (i - 1 + 2 * (i % 2)) % dom_count) for i in range(dom_count)]

    matrix = lane_matrix()
    odd = (lax.axis_index("dom") % 2).astype(jnp.int32).reshape(1)
    comp = lax.axis_index("comp").astype(jnp.int32).reshape(1)
    grid = density[0]
    to_inner, to_outer = send_planes(grid, odd)
    for step in range(STEPS):
        inner = lax.ppermute(to_inner, "dom", inner_pairs)
        outer = lax.ppermute(to_outer, "dom", outer_pairs)
        if step == 0:
            partial, speeds = first_planes(grid, matrix, velocity)
        else:
            partial = advance_planes(grid, matrix, speeds)
        if step < STEPS - 1:
            grid, to_inner, to_outer = edge_planes(odd, partial, inner, outer, speeds)
    cut = Cut(comp_count * dom_count, density.shape[1])
    grid, columns = last_planes(cut, odd, partial, inner, outer, speeds)
    columns, owner_lists = lax.optimization_barrier((columns, owner_lists))
    columns = lax.all_to_all(columns, ("comp", "dom"), 0, 0, tiled=True)
    slabs, partners = merge_tables(owner_lists, comp_count)
    changes = merge_columns(cut, columns, slabs, partners, coefficients, dom_count)
    changes = lax.all_to_all(changes, ("comp", "dom"), 0, 0, tiled=True)
    return final_planes(cut, grid, changes, coefficients, comp)


def solution(mesh):
    in_specs = (
        P("comp", "dom", None, None, None),
        P("comp", None, "dom", None, None, None),
        P(),
        P(),
    )
    out_specs = P("comp", "dom", None, None, None)
    return jax.shard_map(local, mesh=mesh, in_specs=in_specs, out_specs=out_specs, check_vma=False)
```

```python
import functools

import jax
import jax.numpy as jnp
import numpy as np
from jax import lax
from jax.experimental import pallas as pl
from jax.experimental.pallas import tpu as pltpu
from jax.sharding import PartitionSpec as P

GRID_A = 32
GRID_B = 16
GRID_C = 16
LANES = 256
HALF = 128
D_STRIDE = 32
LANE_AXES = ((8, 4), (4, 1))
STEPS = 4
GROUP = 4
SHARED = 4
BORROWED = 4
MULTI = 12
LEVELS = 32000.0
FINE = 16.0
TINY = 1e-36
VMEM_LIMIT = 24 * 1024 * 1024
FIRST_LIMIT = 40 * 1024 * 1024


def params(limit=VMEM_LIMIT):
    return pltpu.CompilerParams(vmem_limit_bytes=limit)


def smem():
    return pl.BlockSpec(memory_space=pltpu.SMEM)


def hbm():
    return pl.BlockSpec(memory_space=pltpu.HBM)


def vmem():
    return pl.BlockSpec(memory_space=pltpu.VMEM)


def code_of(peak):
    return jnp.ceil(jnp.log(jnp.maximum(peak, TINY)) * (FINE / 0.6931471805599453))


def encode(rows, put, put_code):
    peak = jnp.abs(rows[0]())
    for row in rows[1:]:
        peak = jnp.maximum(peak, jnp.abs(row()))
    code = code_of(peak)
    factor = jnp.exp2(code * (-1.0 / FINE)) * LEVELS
    put_code(code.astype(jnp.int32).astype(jnp.int16))
    for index, row in enumerate(rows):
        put(index, jnp.round(row() * factor).astype(jnp.int32).astype(jnp.int16))


def to_float(block):
    return block.astype(jnp.int32).astype(jnp.float32)


def unit_of(code_row):
    return jnp.exp2(to_float(code_row) * (1.0 / FINE)) * (1.0 / LEVELS)


def message_shape():
    return jax.ShapeDtypeStruct((GRID_B + 1, GRID_C, LANES), jnp.int16)


def code_plane(read, target):
    encode(
        [lambda b=b: read(b) for b in range(GRID_B)],
        lambda b, value: target.__setitem__(b, value),
        lambda value: target.__setitem__(GRID_B, value),
    )


def code_edges(odd, grid, inner, outer):
    planes = grid.shape[0]

    def work(to_next, to_last):
        code_plane(lambda b: grid[0, b], to_last)
        code_plane(lambda b: grid[planes - 1, b], to_next)

    @pl.when(odd[0] == 0)
    def _():
        work(inner, outer)

    @pl.when(odd[0] == 1)
    def _():
        work(outer, inner)


def send_planes_body(odd, density, inner, outer, grid):
    del density
    code_edges(odd, grid, inner, outer)


def send_planes(grid, odd):
    return pl.pallas_call(
        send_planes_body,
        in_specs=[smem(), vmem()],
        out_specs=[vmem()] * 3,
        out_shape=[message_shape()] * 2 + [jax.ShapeDtypeStruct(grid.shape, jnp.float32)],
        input_output_aliases={1: 2},
        compiler_params=params(),
    )(odd, grid)


def lane_matrix():
    point = np.arange(LANES)
    eye = np.eye(LANES)
    total = np.zeros((LANES, LANES))
    differences = []
    for extent, stride in LANE_AXES:
        place = point // stride % extent
        forward = eye[:, point + ((place + 1) % extent - place) * stride]
        backward = eye[:, point + ((place - 1) % extent - place) * stride]
        total += forward + backward
        differences.append(forward - backward)
    matrix = np.concatenate([total] + differences, 1)
    return jnp.asarray(np.concatenate([matrix, matrix], 0), jnp.bfloat16)


def lane_products(plane, matrix, products):
    value = plane.reshape(GRID_B * GRID_C, LANES)
    coarse = value.astype(jnp.bfloat16)
    fine = (value - coarse.astype(jnp.float32)).astype(jnp.bfloat16)
    products[...] = jnp.dot(
        jnp.concatenate([coarse, fine], 1), matrix[...], preferred_element_type=jnp.float32
    )


def advance(grid, matrix, speeds, out, even, odd, ready):
    planes = grid.shape[0]

    def rows(plane, products):
        up, down = jnp.minimum(plane + 1, planes - 1), jnp.maximum(plane - 1, 0)
        has_up = jnp.where(plane < planes - 1, 1.0, 0.0)
        has_down = jnp.where(plane > 0, 1.0, 0.0)
        for b in range(GRID_B):
            value = grid[plane, b]
            pairs = [
                (grid[up, b] * has_up, grid[down, b] * has_down),
                (grid[plane, (b + 1) % GRID_B], grid[plane, (b - 1) % GRID_B]),
                (pltpu.roll(value, GRID_C - 1, 0), pltpu.roll(value, 1, 0)),
                (pltpu.roll(value, LANES - D_STRIDE, 1), pltpu.roll(value, D_STRIDE, 1)),
            ]
            place = slice(b * GRID_C, (b + 1) * GRID_C)
            total = products[place, :LANES]
            drift = None
            for d in range(6):
                if d < len(pairs):
                    forward, backward = pairs[d]
                    total = total + (forward + backward)
                    difference = forward - backward
                else:
                    difference = products[place, (d - 3) * LANES : (d - 2) * LANES]
                term = speeds[d, plane, b].astype(jnp.float32) * difference
                drift = term if drift is None else drift + term
            out[plane, b] = 0.28 * value + 0.06 * total - 0.5 * drift

    lane_products(grid[0], matrix, even)

    def pair(index, carry):
        plane = 2 * index
        ready(plane)
        lane_products(grid[plane + 1], matrix, odd)
        rows(plane, even)
        ready(plane + 1)
        lane_products(grid[jnp.minimum(plane + 2, planes - 1)], matrix, even)
        rows(plane + 1, odd)
        return carry

    lax.fori_loop(0, planes // 2, pair, 0)


def advance_body(grid, matrix, speeds, out, even, odd):
    advance(grid, matrix, speeds, out, even, odd, lambda plane: None)


def first_body(grid, matrix, velocity, out, speeds, even, odd, sems):
    planes = grid.shape[0]

    def copy(plane):
        return pltpu.make_async_copy(velocity.at[0, :, plane], speeds.at[:, plane], sems.at[plane])

    for plane in range(planes):
        copy(plane).start()
    advance(grid, matrix, speeds, out, even, odd, lambda plane: copy(plane).wait())


def first_planes(grid, matrix, velocity):
    products = pltpu.VMEM((GRID_B * GRID_C, matrix.shape[1]), jnp.float32)
    return pl.pallas_call(
        first_body,
        in_specs=[vmem(), vmem(), hbm()],
        out_specs=[vmem()] * 2,
        out_shape=[
            jax.ShapeDtypeStruct(grid.shape, jnp.float32),
            jax.ShapeDtypeStruct(velocity.shape[1:], jnp.bfloat16),
        ],
        scratch_shapes=[products, products, pltpu.SemaphoreType.DMA((grid.shape[0],))],
        compiler_params=params(FIRST_LIMIT),
        cost_estimate=pl.CostEstimate(
            flops=1000 * grid.size, bytes_accessed=20 * grid.size, transcendentals=0
        ),
    )(grid, matrix, velocity)


def advance_planes(grid, matrix, velocity):
    points = grid.size
    products = pltpu.VMEM((GRID_B * GRID_C, matrix.shape[1]), jnp.float32)
    return pl.pallas_call(
        advance_body,
        in_specs=[vmem()] * 3,
        out_specs=vmem(),
        out_shape=jax.ShapeDtypeStruct(grid.shape, jnp.float32),
        scratch_shapes=[products, products],
        compiler_params=params(),
        cost_estimate=pl.CostEstimate(
            flops=1000 * points, bytes_accessed=20 * points, transcendentals=0
        ),
    )(grid, matrix, velocity)


def add_edges(odd, inner, outer, speeds, out):
    planes = out.shape[0]

    def work(from_next, from_last):
        for plane, source, sign in ((0, from_last, 0.5), (planes - 1, from_next, -0.5)):
            unit = unit_of(source[GRID_B])
            for b in range(GRID_B):
                share = 0.06 + sign * speeds[0, plane, b].astype(jnp.float32)
                out[plane, b] = out[plane, b] + to_float(source[b]) * unit * share

    @pl.when(odd[0] == 0)
    def _():
        work(inner, outer)

    @pl.when(odd[0] == 1)
    def _():
        work(outer, inner)


def edge_body(odd, partial, inner, outer, speeds, out, to_inner, to_outer):
    del partial
    add_edges(odd, inner, outer, speeds, out)
    code_edges(odd, out, to_inner, to_outer)


def edge_planes(odd, partial, inner, outer, speeds):
    return pl.pallas_call(
        edge_body,
        in_specs=[smem()] + [vmem()] * 4,
        out_specs=[vmem()] * 3,
        out_shape=[jax.ShapeDtypeStruct(partial.shape, jnp.float32)] + [message_shape()] * 2,
        input_output_aliases={1: 0},
        compiler_params=params(),
        cost_estimate=pl.CostEstimate(
            flops=2_000_000, bytes_accessed=2_000_000, transcendentals=0
        ),
    )(odd, partial, inner, outer, speeds)


class Cut:
    def __init__(self, count, planes):
        self.count, self.planes = count, planes
        self.splits = count // (2 * GRID_B)
        self.extent = GRID_C // self.splits
        self.code_rows = min(self.extent, 8)
        self.groups = self.extent // self.code_rows
        self.data_rows = planes * self.extent
        self.stack = min(planes, max(1, 16 // self.extent))
        self.per_row = 2 * self.splits

    def shape(self):
        return jax.ShapeDtypeStruct(
            (self.count, self.data_rows + self.code_rows, HALF), jnp.int16
        )

    def place(self, chunk):
        half, part = divmod(chunk, self.splits)
        return (
            slice(part * self.extent, (part + 1) * self.extent),
            slice(half * HALF, (half + 1) * HALF),
        )

    def spread(self, tile, repeats=1):
        return jnp.concatenate([tile] * (self.groups * repeats), 0)

    def put(self, target, chunk, value_of):
        peak = jnp.abs(value_of(0))
        for plane in range(1, self.planes):
            peak = jnp.maximum(peak, jnp.abs(value_of(plane)))
        top = peak[: self.code_rows]
        for group in range(1, self.groups):
            top = jnp.maximum(top, peak[group * self.code_rows : (group + 1) * self.code_rows])
        code = code_of(top)
        factor = self.spread(jnp.exp2(code * (-1.0 / FINE)) * LEVELS, self.stack)
        size = self.stack * self.extent
        for index in range(0, self.planes, self.stack):
            block = jnp.concatenate([value_of(index + i) for i in range(self.stack)], 0)
            start = index * self.extent
            target[chunk, start : start + size] = (
                jnp.round(block * factor).astype(jnp.int32).astype(jnp.int16)
            )
        target[chunk, self.data_rows :] = code.astype(jnp.int32).astype(jnp.int16)

    def values(self, source, chunk):
        unit = self.spread(unit_of(source[chunk, self.data_rows :]), self.stack)
        values = []
        size = self.stack * self.extent
        for index in range(0, self.planes, self.stack):
            start = index * self.extent
            block = to_float(source[chunk, start : start + size]) * unit
            for i in range(self.stack):
                values.append(block[i * self.extent : (i + 1) * self.extent])
        return values


def last_body(cut, odd, partial, inner, outer, speeds, grid, out):
    del partial
    add_edges(odd, inner, outer, speeds, grid)

    def pack(index, carry):
        for row in range(GROUP):
            b = index * GROUP + row
            for chunk in range(cut.per_row):
                place = cut.place(chunk)
                cut.put(out, b * cut.per_row + chunk, lambda p: grid[(p, b) + place])
        return carry

    lax.fori_loop(0, GRID_B // GROUP, pack, 0)


def last_planes(cut, odd, partial, inner, outer, speeds):
    return pl.pallas_call(
        functools.partial(last_body, cut),
        in_specs=[smem()] + [vmem()] * 4,
        out_specs=[vmem()] * 2,
        out_shape=[jax.ShapeDtypeStruct(partial.shape, jnp.float32), cut.shape()],
        input_output_aliases={1: 0},
        compiler_params=params(),
    )(odd, partial, inner, outer, speeds)


def merge_body(
    cut, dom_count, table, weights, columns, out, values, rows, sums, grid
):
    comp_count = cut.count // dom_count

    def unpack(source, carry):
        for plane, value in enumerate(cut.values(columns, source)):
            values[source * cut.planes + plane] = value
        return carry

    lax.fori_loop(0, cut.count, unpack, 0, unroll=2)

    def gather(comp, carry):
        weight = weights[comp].astype(jnp.float32)
        base = comp * GRID_A
        for index in range(MULTI):
            slab = table[comp, index]
            spacing = slab & -slab
            share = jnp.where(slab > 0, -0.5 * weight, 0.0)
            near = (
                values[base + ((slab - spacing) & (GRID_A - 1))]
                + values[base + ((slab + spacing) & (GRID_A - 1))]
            )
            rows[comp * MULTI + index] = values[base + slab] * weight + near * share
        return carry

    lax.fori_loop(0, comp_count, gather, 0)
    for index in range(SHARED):
        total = rows[index]
        for comp in range(1, comp_count):
            total = total + rows[comp * MULTI + index]
        sums[index] = total
    grid[...] = jnp.zeros_like(grid)

    def scatter(comp, carry):
        for index in range(MULTI):
            if index < SHARED:
                change = sums[index] - rows[comp * MULTI + index]
            else:
                change = rows[table[comp, MULTI + index]]
            grid[comp, table[comp, index]] = change
        return carry

    lax.fori_loop(0, comp_count, scatter, 0)

    def send(comp, carry):
        nodal = [grid[comp, position] for position in range(GRID_A)]
        spacing = GRID_A // 2
        while spacing >= 1:
            for position in range(spacing, GRID_A, 2 * spacing):
                nodal[position] = nodal[position] + 0.5 * (
                    nodal[position - spacing] + nodal[(position + spacing) % GRID_A]
                )
            spacing //= 2
        for dom in range(dom_count):
            cut.put(out, comp * dom_count + dom, lambda p: nodal[dom * cut.planes + p])
        return carry

    lax.fori_loop(0, comp_count, send, 0)


def merge_columns(cut, columns, table, weights, dom_count):
    comp_count = cut.count // dom_count
    tile = (cut.extent, HALF)
    return pl.pallas_call(
        functools.partial(merge_body, cut, dom_count),
        in_specs=[smem()] * 2 + [vmem()],
        out_specs=vmem(),
        out_shape=cut.shape(),
        scratch_shapes=[
            pltpu.VMEM((comp_count * GRID_A,) + tile, jnp.float32),
            pltpu.VMEM((comp_count * MULTI,) + tile, jnp.float32),
            pltpu.VMEM((SHARED,) + tile, jnp.float32),
            pltpu.VMEM((comp_count, GRID_A) + tile, jnp.float32),
        ],
        compiler_params=params(),
    )(table, weights, columns)


def final_body(cut, weight, grid, changes, out, stage, sems):
    def copy(index):
        span = pl.ds(index * GROUP, GROUP)
        return pltpu.make_async_copy(stage.at[:, span], out.at[0, :, span], sems.at[index])

    def combine(index, carry):
        for row in range(GROUP):
            b = index * GROUP + row
            for chunk in range(cut.per_row):
                place = cut.place(chunk)
                for p, value in enumerate(cut.values(changes, b * cut.per_row + chunk)):
                    stage[(p, b) + place] = grid[(p, b) + place] * weight[0] + value
        copy(index).start()
        return carry

    lax.fori_loop(0, GRID_B // GROUP, combine, 0)
    for index in range(GRID_B // GROUP):
        copy(index).wait()


def final_planes(cut, grid, changes, weight):
    return pl.pallas_call(
        functools.partial(final_body, cut),
        in_specs=[smem(), vmem(), vmem()],
        out_specs=hbm(),
        out_shape=jax.ShapeDtypeStruct((1,) + grid.shape, jnp.float32),
        scratch_shapes=[
            pltpu.VMEM(grid.shape, jnp.float32),
            pltpu.SemaphoreType.DMA((GRID_B // GROUP,)),
        ],
        compiler_params=params(),
    )(weight, grid, changes)


def tables_body(owners, table, places):
    blocks = owners.shape[0]
    comp_count = table.shape[0]

    def clear(comp, carry):
        places[comp] = SHARED
        for index in range(SHARED):
            table[comp, MULTI + index] = 0
        return carry

    lax.fori_loop(0, comp_count, clear, 0)

    def block(number, shared):
        first, second = owners[number, 0], owners[number, 1]
        is_shared = owners[number, 2] >= 0

        @pl.when((second >= 0) & ~is_shared)
        def _():
            comps = [lax.div(slab, GRID_A) for slab in (first, second)]
            own = [places[comp] for comp in comps]
            for side, slab in enumerate((first, second)):
                table[comps[side], own[side]] = lax.rem(slab, GRID_A)
                partner = comps[1 - side] * MULTI + own[1 - side]
                table[comps[side], MULTI + own[side]] = partner
                places[comps[side]] = own[side] + 1

        @pl.when(is_shared)
        def _():
            def holder(index, carry):
                slab = owners[number, index]
                table[lax.div(slab, GRID_A), shared] = lax.rem(slab, GRID_A)
                return carry

            lax.fori_loop(0, comp_count, holder, 0)

        return shared + jnp.where(is_shared, 1, 0)

    lax.fori_loop(0, blocks, block, 0)


def merge_tables(owner_lists, comp_count):
    return pl.pallas_call(
        tables_body,
        in_specs=[smem()],
        out_specs=smem(),
        out_shape=jax.ShapeDtypeStruct((comp_count, 2 * MULTI), jnp.int32),
        scratch_shapes=[pltpu.SMEM((comp_count,), jnp.int32)],
    )(owner_lists)


def local(density, velocity, coefficients, owner_lists):
    comp_count, dom_count = lax.axis_size("comp"), lax.axis_size("dom")
    inner_pairs = [(i, i ^ 1) for i in range(dom_count)]
    outer_pairs = [(i, (i - 1 + 2 * (i % 2)) % dom_count) for i in range(dom_count)]

    matrix = lane_matrix()
    odd = (lax.axis_index("dom") % 2).astype(jnp.int32).reshape(1)
    to_inner, to_outer, grid = send_planes(density[0], odd)
    for step in range(STEPS):
        inner = lax.ppermute(to_inner, "dom", inner_pairs)
        outer = lax.ppermute(to_outer, "dom", outer_pairs)
        if step == 0:
            partial, speeds = first_planes(grid, matrix, velocity)
        else:
            partial = advance_planes(grid, matrix, speeds)
        if step < STEPS - 1:
            grid, to_inner, to_outer = edge_planes(odd, partial, inner, outer, speeds)
    cut = Cut(comp_count * dom_count, density.shape[1])
    grid, columns = last_planes(cut, odd, partial, inner, outer, speeds)
    columns, owner_lists = lax.optimization_barrier((columns, owner_lists))
    columns = lax.all_to_all(columns, ("comp", "dom"), 0, 0, tiled=True)
    table = merge_tables(owner_lists, comp_count)
    changes = merge_columns(cut, columns, table, coefficients, dom_count)
    changes, coefficients = lax.optimization_barrier((changes, coefficients))
    weight = lax.dynamic_slice_in_dim(coefficients, lax.axis_index("comp"), 1).astype(jnp.float32)
    changes = lax.all_to_all(changes, ("comp", "dom"), 0, 0, tiled=True)
    return final_planes(cut, grid, changes, weight)


def solution(mesh):
    in_specs = (
        P("comp", "dom", None, None, None),
        P("comp", None, "dom", None, None, None),
        P(),
        P(),
    )
    out_specs = P("comp", "dom", None, None, None)
    return jax.shard_map(local, mesh=mesh, in_specs=in_specs, out_specs=out_specs, check_vma=False)
```

```python
import functools

import jax
import jax.numpy as jnp
import numpy as np
from jax import lax
from jax.experimental import pallas as pl
from jax.experimental.pallas import tpu as pltpu
from jax.sharding import PartitionSpec as P

GRID_A = 32
GRID_B = 16
GRID_C = 16
LANES = 256
HALF = 128
D_STRIDE = 32
LANE_AXES = ((8, 4), (4, 1))
STEPS = 4
GROUP = 4
SHARED = 4
BORROWED = 4
MULTI = 12
LEVELS = 32000.0
FINE = 16.0
TINY = 1e-36
VMEM_LIMIT = 24 * 1024 * 1024
FIRST_LIMIT = 40 * 1024 * 1024


def params(limit=VMEM_LIMIT):
    return pltpu.CompilerParams(vmem_limit_bytes=limit)


def smem():
    return pl.BlockSpec(memory_space=pltpu.SMEM)


def hbm():
    return pl.BlockSpec(memory_space=pltpu.HBM)


def vmem():
    return pl.BlockSpec(memory_space=pltpu.VMEM)


def code_of(peak):
    return jnp.ceil(jnp.log(jnp.maximum(peak, TINY)) * (FINE / 0.6931471805599453))


def encode(rows, put, put_code):
    peak = jnp.abs(rows[0]())
    for row in rows[1:]:
        peak = jnp.maximum(peak, jnp.abs(row()))
    code = code_of(peak)
    factor = jnp.exp2(code * (-1.0 / FINE)) * LEVELS
    put_code(code.astype(jnp.int32).astype(jnp.int16))
    for index, row in enumerate(rows):
        put(index, jnp.round(row() * factor).astype(jnp.int32).astype(jnp.int16))


def to_float(block):
    return block.astype(jnp.int32).astype(jnp.float32)


def unit_of(code_row):
    return jnp.exp2(to_float(code_row) * (1.0 / FINE)) * (1.0 / LEVELS)


def message_shape():
    return jax.ShapeDtypeStruct((GRID_B + 1, GRID_C, LANES), jnp.int16)


def code_plane(read, target):
    encode(
        [lambda b=b: read(b) for b in range(GRID_B)],
        lambda b, value: target.__setitem__(b, value),
        lambda value: target.__setitem__(GRID_B, value),
    )


def code_edges(odd, grid, inner, outer):
    planes = grid.shape[0]

    def work(to_next, to_last):
        code_plane(lambda b: grid[0, b], to_last)
        code_plane(lambda b: grid[planes - 1, b], to_next)

    @pl.when(odd[0] == 0)
    def _():
        work(inner, outer)

    @pl.when(odd[0] == 1)
    def _():
        work(outer, inner)


def send_planes_body(odd, density, inner, outer, grid):
    del density
    code_edges(odd, grid, inner, outer)


def send_planes(grid, odd):
    return pl.pallas_call(
        send_planes_body,
        in_specs=[smem(), vmem()],
        out_specs=[vmem()] * 3,
        out_shape=[message_shape()] * 2 + [jax.ShapeDtypeStruct(grid.shape, jnp.float32)],
        input_output_aliases={1: 2},
        compiler_params=params(),
    )(odd, grid)


def lane_matrix():
    point = np.arange(LANES)
    eye = np.eye(LANES)
    total = np.zeros((LANES, LANES))
    differences = []
    for extent, stride in LANE_AXES:
        place = point // stride % extent
        forward = eye[:, point + ((place + 1) % extent - place) * stride]
        backward = eye[:, point + ((place - 1) % extent - place) * stride]
        total += forward + backward
        differences.append(forward - backward)
    matrix = np.concatenate([total] + differences, 1)
    return jnp.asarray(np.concatenate([matrix, matrix], 0), jnp.bfloat16)


def lane_products(plane, matrix, products):
    value = plane.reshape(GRID_B * GRID_C, LANES)
    coarse = value.astype(jnp.bfloat16)
    fine = (value - coarse.astype(jnp.float32)).astype(jnp.bfloat16)
    products[...] = jnp.dot(
        jnp.concatenate([coarse, fine], 1), matrix[...], preferred_element_type=jnp.float32
    )


def advance(grid, matrix, speeds, out, even, odd, ready):
    planes = grid.shape[0]

    def rows(plane, products):
        up, down = jnp.minimum(plane + 1, planes - 1), jnp.maximum(plane - 1, 0)
        has_up = jnp.where(plane < planes - 1, 1.0, 0.0)
        has_down = jnp.where(plane > 0, 1.0, 0.0)
        for b in range(GRID_B):
            value = grid[plane, b]
            pairs = [
                (grid[up, b] * has_up, grid[down, b] * has_down),
                (grid[plane, (b + 1) % GRID_B], grid[plane, (b - 1) % GRID_B]),
                (pltpu.roll(value, GRID_C - 1, 0), pltpu.roll(value, 1, 0)),
                (pltpu.roll(value, LANES - D_STRIDE, 1), pltpu.roll(value, D_STRIDE, 1)),
            ]
            place = slice(b * GRID_C, (b + 1) * GRID_C)
            total = products[place, :LANES]
            drift = None
            for d in range(6):
                if d < len(pairs):
                    forward, backward = pairs[d]
                    total = total + (forward + backward)
                    difference = forward - backward
                else:
                    difference = products[place, (d - 3) * LANES : (d - 2) * LANES]
                term = speeds[d, plane, b].astype(jnp.float32) * difference
                drift = term if drift is None else drift + term
            out[plane, b] = 0.28 * value + 0.06 * total - 0.5 * drift

    lane_products(grid[0], matrix, even)

    def pair(index, carry):
        plane = 2 * index
        ready(plane)
        lane_products(grid[plane + 1], matrix, odd)
        rows(plane, even)
        ready(plane + 1)
        lane_products(grid[jnp.minimum(plane + 2, planes - 1)], matrix, even)
        rows(plane + 1, odd)
        return carry

    lax.fori_loop(0, planes // 2, pair, 0)


def advance_body(grid, matrix, speeds, out, even, odd):
    advance(grid, matrix, speeds, out, even, odd, lambda plane: None)


def first_body(grid, matrix, velocity, out, speeds, even, odd, sems):
    planes = grid.shape[0]

    def copy(plane):
        return pltpu.make_async_copy(velocity.at[0, :, plane], speeds.at[:, plane], sems.at[plane])

    for plane in range(planes):
        copy(plane).start()
    advance(grid, matrix, speeds, out, even, odd, lambda plane: copy(plane).wait())


def first_planes(grid, matrix, velocity):
    products = pltpu.VMEM((GRID_B * GRID_C, matrix.shape[1]), jnp.float32)
    return pl.pallas_call(
        first_body,
        in_specs=[vmem(), vmem(), hbm()],
        out_specs=[vmem()] * 2,
        out_shape=[
            jax.ShapeDtypeStruct(grid.shape, jnp.float32),
            jax.ShapeDtypeStruct(velocity.shape[1:], jnp.bfloat16),
        ],
        scratch_shapes=[products, products, pltpu.SemaphoreType.DMA((grid.shape[0],))],
        compiler_params=params(FIRST_LIMIT),
        cost_estimate=pl.CostEstimate(
            flops=1000 * grid.size, bytes_accessed=20 * grid.size, transcendentals=0
        ),
    )(grid, matrix, velocity)


def advance_planes(grid, matrix, velocity):
    points = grid.size
    products = pltpu.VMEM((GRID_B * GRID_C, matrix.shape[1]), jnp.float32)
    return pl.pallas_call(
        advance_body,
        in_specs=[vmem()] * 3,
        out_specs=vmem(),
        out_shape=jax.ShapeDtypeStruct(grid.shape, jnp.float32),
        scratch_shapes=[products, products],
        compiler_params=params(),
        cost_estimate=pl.CostEstimate(
            flops=1000 * points, bytes_accessed=20 * points, transcendentals=0
        ),
    )(grid, matrix, velocity)


def add_edges(odd, inner, outer, speeds, out):
    planes = out.shape[0]

    def work(from_next, from_last):
        for plane, source, sign in ((0, from_last, 0.5), (planes - 1, from_next, -0.5)):
            unit = unit_of(source[GRID_B])
            for b in range(GRID_B):
                share = 0.06 + sign * speeds[0, plane, b].astype(jnp.float32)
                out[plane, b] = out[plane, b] + to_float(source[b]) * unit * share

    @pl.when(odd[0] == 0)
    def _():
        work(inner, outer)

    @pl.when(odd[0] == 1)
    def _():
        work(outer, inner)


def edge_body(odd, partial, inner, outer, speeds, out, to_inner, to_outer):
    del partial
    add_edges(odd, inner, outer, speeds, out)
    code_edges(odd, out, to_inner, to_outer)


def edge_planes(odd, partial, inner, outer, speeds):
    return pl.pallas_call(
        edge_body,
        in_specs=[smem()] + [vmem()] * 4,
        out_specs=[vmem()] * 3,
        out_shape=[jax.ShapeDtypeStruct(partial.shape, jnp.float32)] + [message_shape()] * 2,
        input_output_aliases={1: 0},
        compiler_params=params(),
        cost_estimate=pl.CostEstimate(
            flops=2_000_000, bytes_accessed=2_000_000, transcendentals=0
        ),
    )(odd, partial, inner, outer, speeds)


class Cut:
    def __init__(self, count, planes):
        self.count, self.planes = count, planes
        self.splits = count // (2 * GRID_B)
        self.extent = GRID_C // self.splits
        self.code_rows = min(self.extent, 8)
        self.groups = self.extent // self.code_rows
        self.data_rows = planes * self.extent
        self.stack = min(planes, max(1, 16 // self.extent))
        self.per_row = 2 * self.splits

    def shape(self):
        return jax.ShapeDtypeStruct(
            (self.count, self.data_rows + self.code_rows, HALF), jnp.int16
        )

    def place(self, chunk):
        half, part = divmod(chunk, self.splits)
        return (
            slice(part * self.extent, (part + 1) * self.extent),
            slice(half * HALF, (half + 1) * HALF),
        )

    def spread(self, tile, repeats=1):
        return jnp.concatenate([tile] * (self.groups * repeats), 0)

    def put(self, target, chunk, value_of):
        peak = jnp.abs(value_of(0))
        for plane in range(1, self.planes):
            peak = jnp.maximum(peak, jnp.abs(value_of(plane)))
        top = peak[: self.code_rows]
        for group in range(1, self.groups):
            top = jnp.maximum(top, peak[group * self.code_rows : (group + 1) * self.code_rows])
        code = code_of(top)
        factor = self.spread(jnp.exp2(code * (-1.0 / FINE)) * LEVELS, self.stack)
        size = self.stack * self.extent
        for index in range(0, self.planes, self.stack):
            block = jnp.concatenate([value_of(index + i) for i in range(self.stack)], 0)
            start = index * self.extent
            target[chunk, start : start + size] = (
                jnp.round(block * factor).astype(jnp.int32).astype(jnp.int16)
            )
        target[chunk, self.data_rows :] = code.astype(jnp.int32).astype(jnp.int16)

    def values(self, source, chunk):
        unit = self.spread(unit_of(source[chunk, self.data_rows :]), self.stack)
        values = []
        size = self.stack * self.extent
        for index in range(0, self.planes, self.stack):
            start = index * self.extent
            block = to_float(source[chunk, start : start + size]) * unit
            for i in range(self.stack):
                values.append(block[i * self.extent : (i + 1) * self.extent])
        return values


def last_body(cut, odd, partial, inner, outer, speeds, grid, out):
    del partial
    add_edges(odd, inner, outer, speeds, grid)

    def pack(index, carry):
        for row in range(GROUP):
            b = index * GROUP + row
            for chunk in range(cut.per_row):
                place = cut.place(chunk)
                cut.put(out, b * cut.per_row + chunk, lambda p: grid[(p, b) + place])
        return carry

    lax.fori_loop(0, GRID_B // GROUP, pack, 0)


def last_planes(cut, odd, partial, inner, outer, speeds):
    return pl.pallas_call(
        functools.partial(last_body, cut),
        in_specs=[smem()] + [vmem()] * 4,
        out_specs=[vmem()] * 2,
        out_shape=[jax.ShapeDtypeStruct(partial.shape, jnp.float32), cut.shape()],
        input_output_aliases={1: 0},
        compiler_params=params(),
    )(odd, partial, inner, outer, speeds)


def merge_body(
    cut, dom_count, table, weights, columns, out, values, rows, sums, grid
):
    comp_count = cut.count // dom_count

    def unpack(source, carry):
        for plane, value in enumerate(cut.values(columns, source)):
            values[source * cut.planes + plane] = value
        return carry

    lax.fori_loop(0, cut.count, unpack, 0, unroll=4)

    def gather(comp, carry):
        weight = weights[comp].astype(jnp.float32)
        base = comp * GRID_A
        for index in range(MULTI):
            slab = table[comp, index]
            spacing = slab & -slab
            share = jnp.where(slab > 0, -0.5 * weight, 0.0)
            near = (
                values[base + ((slab - spacing) & (GRID_A - 1))]
                + values[base + ((slab + spacing) & (GRID_A - 1))]
            )
            rows[comp * MULTI + index] = values[base + slab] * weight + near * share
        return carry

    lax.fori_loop(0, comp_count, gather, 0, unroll=2)
    for index in range(SHARED):
        total = rows[index]
        for comp in range(1, comp_count):
            total = total + rows[comp * MULTI + index]
        sums[index] = total
    grid[...] = jnp.zeros_like(grid)

    def scatter(comp, carry):
        for index in range(MULTI):
            if index < SHARED:
                change = sums[index] - rows[comp * MULTI + index]
            else:
                change = rows[table[comp, MULTI + index]]
            grid[comp, table[comp, index]] = change
        return carry

    lax.fori_loop(0, comp_count, scatter, 0)

    def send(comp, carry):
        nodal = [grid[comp, position] for position in range(GRID_A)]
        spacing = GRID_A // 2
        while spacing >= 1:
            for position in range(spacing, GRID_A, 2 * spacing):
                nodal[position] = nodal[position] + 0.5 * (
                    nodal[position - spacing] + nodal[(position + spacing) % GRID_A]
                )
            spacing //= 2
        for dom in range(dom_count):
            cut.put(out, comp * dom_count + dom, lambda p: nodal[dom * cut.planes + p])
        return carry

    lax.fori_loop(0, comp_count, send, 0, unroll=2)


def merge_columns(cut, columns, table, weights, dom_count):
    comp_count = cut.count // dom_count
    tile = (cut.extent, HALF)
    return pl.pallas_call(
        functools.partial(merge_body, cut, dom_count),
        in_specs=[smem()] * 2 + [vmem()],
        out_specs=vmem(),
        out_shape=cut.shape(),
        scratch_shapes=[
            pltpu.VMEM((comp_count * GRID_A,) + tile, jnp.float32),
            pltpu.VMEM((comp_count * MULTI,) + tile, jnp.float32),
            pltpu.VMEM((SHARED,) + tile, jnp.float32),
            pltpu.VMEM((comp_count, GRID_A) + tile, jnp.float32),
        ],
        compiler_params=params(),
    )(table, weights, columns)


def final_body(cut, weight, grid, changes, out, stage, sems):
    def copy(index):
        span = pl.ds(index * GROUP, GROUP)
        return pltpu.make_async_copy(stage.at[:, span], out.at[0, :, span], sems.at[index])

    def combine(index, carry):
        for row in range(GROUP):
            b = index * GROUP + row
            for chunk in range(cut.per_row):
                place = cut.place(chunk)
                for p, value in enumerate(cut.values(changes, b * cut.per_row + chunk)):
                    stage[(p, b) + place] = grid[(p, b) + place] * weight[0] + value
        copy(index).start()
        return carry

    lax.fori_loop(0, GRID_B // GROUP, combine, 0)
    for index in range(GRID_B // GROUP):
        copy(index).wait()


def final_planes(cut, grid, changes, weight):
    return pl.pallas_call(
        functools.partial(final_body, cut),
        in_specs=[smem(), vmem(), vmem()],
        out_specs=hbm(),
        out_shape=jax.ShapeDtypeStruct((1,) + grid.shape, jnp.float32),
        scratch_shapes=[
            pltpu.VMEM(grid.shape, jnp.float32),
            pltpu.SemaphoreType.DMA((GRID_B // GROUP,)),
        ],
        compiler_params=params(),
    )(weight, grid, changes)


def tables_body(owners, table, places):
    blocks = owners.shape[0]
    comp_count = table.shape[0]

    def clear(comp, carry):
        places[comp] = SHARED
        for index in range(SHARED):
            table[comp, MULTI + index] = 0
        return carry

    lax.fori_loop(0, comp_count, clear, 0)

    def block(number, shared):
        first, second = owners[number, 0], owners[number, 1]
        is_shared = owners[number, 2] >= 0

        @pl.when((second >= 0) & ~is_shared)
        def _():
            comps = [lax.div(slab, GRID_A) for slab in (first, second)]
            own = [places[comp] for comp in comps]
            for side, slab in enumerate((first, second)):
                table[comps[side], own[side]] = lax.rem(slab, GRID_A)
                partner = comps[1 - side] * MULTI + own[1 - side]
                table[comps[side], MULTI + own[side]] = partner
                places[comps[side]] = own[side] + 1

        @pl.when(is_shared)
        def _():
            def holder(index, carry):
                slab = owners[number, index]
                table[lax.div(slab, GRID_A), shared] = lax.rem(slab, GRID_A)
                return carry

            lax.fori_loop(0, comp_count, holder, 0)

        return shared + jnp.where(is_shared, 1, 0)

    lax.fori_loop(0, blocks, block, 0)


def merge_tables(owner_lists, comp_count):
    return pl.pallas_call(
        tables_body,
        in_specs=[smem()],
        out_specs=smem(),
        out_shape=jax.ShapeDtypeStruct((comp_count, 2 * MULTI), jnp.int32),
        scratch_shapes=[pltpu.SMEM((comp_count,), jnp.int32)],
    )(owner_lists)


def local(density, velocity, coefficients, owner_lists):
    comp_count, dom_count = lax.axis_size("comp"), lax.axis_size("dom")
    inner_pairs = [(i, i ^ 1) for i in range(dom_count)]
    outer_pairs = [(i, (i - 1 + 2 * (i % 2)) % dom_count) for i in range(dom_count)]

    matrix = lane_matrix()
    odd = (lax.axis_index("dom") % 2).astype(jnp.int32).reshape(1)
    to_inner, to_outer, grid = send_planes(density[0], odd)
    for step in range(STEPS):
        inner = lax.ppermute(to_inner, "dom", inner_pairs)
        outer = lax.ppermute(to_outer, "dom", outer_pairs)
        if step == 0:
            partial, speeds = first_planes(grid, matrix, velocity)
        else:
            partial = advance_planes(grid, matrix, speeds)
        if step < STEPS - 1:
            grid, to_inner, to_outer = edge_planes(odd, partial, inner, outer, speeds)
    cut = Cut(comp_count * dom_count, density.shape[1])
    grid, columns = last_planes(cut, odd, partial, inner, outer, speeds)
    columns, owner_lists = lax.optimization_barrier((columns, owner_lists))
    columns = lax.all_to_all(columns, ("comp", "dom"), 0, 0, tiled=True)
    table = merge_tables(owner_lists, comp_count)
    changes = merge_columns(cut, columns, table, coefficients, dom_count)
    changes, coefficients = lax.optimization_barrier((changes, coefficients))
    weight = lax.dynamic_slice_in_dim(coefficients, lax.axis_index("comp"), 1).astype(jnp.float32)
    changes = lax.all_to_all(changes, ("comp", "dom"), 0, 0, tiled=True)
    return final_planes(cut, grid, changes, weight)


def solution(mesh):
    in_specs = (
        P("comp", "dom", None, None, None),
        P("comp", None, "dom", None, None, None),
        P(),
        P(),
    )
    out_specs = P("comp", "dom", None, None, None)
    return jax.shard_map(local, mesh=mesh, in_specs=in_specs, out_specs=out_specs, check_vma=False)
```
